256 devices in a mesh: ctx: 8 (over y_lo, x), resp: 32 (over y_hi, z, core).
Axes of the slice: x: 4, y: 4 (y_hi: 2, y_lo: 2; y = y_hi * 2 + y_lo), z: 8, core: 2. Of those that a mesh axis runs over, the one named last changes fastest.
Arguments:
- resp_query: bfloat16 [32, 1024, 4096], P('resp', 'ctx'), may hold values from -10 to 10
- resp_key: bfloat16 [32, 1024, 512], P('resp', 'ctx'), may hold values from -5 to 5
- resp_value: bfloat16 [32, 1024, 512], P('resp', 'ctx'), may hold values from -6 to 6
- resp_out: bfloat16 [32, 1024, 4096], P('resp', 'ctx'), may hold values from -3 to 3
- resp_grad: bfloat16 [32, 1024, 4096], P('resp', 'ctx'), may hold values from -6 to 6
- pack_query: bfloat16 [512, 4096], P(('ctx', 'resp')), may hold values from -10 to 10
- pack_key: bfloat16 [512, 512], P(('ctx', 'resp')), may hold values from -5 to 5
- pack_value: bfloat16 [512, 512], P(('ctx', 'resp')), may hold values from -6 to 6
- pack_out: bfloat16 [512, 4096], P(('ctx', 'resp')), may hold values from -3 to 3
- pack_grad: bfloat16 [512, 4096], P(('ctx', 'resp')), may hold values from -6 to 6
- resp_length: int32 [32], P('resp'), may hold values from 1 to 1024, as said below
- prompt_id: int32 [32], P('resp'), may hold values from 0 to 1
- pack_offset: int32 [3], replicated, may hold values from 0 to 512, as said below
Outputs:
- resp_query_grad: bfloat16 [32, 1024, 4096], P('resp', 'ctx')
- resp_key_grad: bfloat16 [32, 1024, 512], P('resp', 'ctx')
- resp_value_grad: bfloat16 [32, 1024, 512], P('resp', 'ctx')
- pack_query_grad: bfloat16 [512, 4096], P(('ctx', 'resp'))
- pack_key_grad: bfloat16 [512, 512], P(('ctx', 'resp'))
- pack_value_grad: bfloat16 [512, 512], P(('ctx', 'resp'))
The draws below stay inside these ranges and needn't reach their ends.
Inputs may be any that keep to these rules, and one draw needn't show every extreme that they name: pack_offset starts at 0, rises strictly and ends at 512. `resp_length`: some response has the full length 1024.
All inputs are finite; a program needn't handle non-finite values.
Results may differ from the reference program's by a relative error of at most 0.015.
Values may be sent and summed in bfloat16 or wider, within the bound.
No kernel may reach another device: no remote copies, remote signals or barrier semaphores. Data moves between devices by JAX's collectives and lax.ppermute only.
A program may use at most 128 MiB of HBM per device.

```python
import jax
import jax.numpy as jnp
from jax import lax

HQ = 32
KEY_VALUE_HEADS = 4
HEAD_SIZE = 128
PROMPTS = 2
R_DEV = 128
RESPS = 32
RESPONSE_LENGTH = 1024
PROMPT_PACK_LEN = 512
N_CTX = 8


def draw_resp_query(key, part):
    key = jax.random.fold_in(key, 11)
    array_shape = (RESPS, RESPONSE_LENGTH, HQ * HEAD_SIZE)
    values_out = jnp.clip(jax.random.normal(key, array_shape, jnp.float32) * 1.5, -9.0, 9.0)
    return values_out.astype(jnp.bfloat16)


def draw_pack_query(key, part):
    key = jax.random.fold_in(key, 12)
    array_shape = (PROMPT_PACK_LEN, HQ * HEAD_SIZE)
    values_out = jnp.clip(jax.random.normal(key, array_shape, jnp.float32) * 1.5, -9.0, 9.0)
    return values_out.astype(jnp.bfloat16)


def draw_resp_key(key, part):
    key = jax.random.fold_in(key, 13)
    array_shape = (RESPS, RESPONSE_LENGTH, KEY_VALUE_HEADS * HEAD_SIZE)
    values_out = jnp.clip(jax.random.normal(key, array_shape, jnp.float32), -5.0, 5.0)
    return values_out.astype(jnp.bfloat16)


def draw_pack_key(key, part):
    key = jax.random.fold_in(key, 14)
    array_shape = (PROMPT_PACK_LEN, KEY_VALUE_HEADS * HEAD_SIZE)
    values_out = jnp.clip(jax.random.normal(key, array_shape, jnp.float32), -5.0, 5.0)
    return values_out.astype(jnp.bfloat16)


def draw_resp_length(key, part):
    key = jax.random.fold_in(key, 15)
    lengths = jax.random.randint(key, (RESPS,), 1, RESPONSE_LENGTH + 1, dtype=jnp.int32)
    chosen = jax.random.randint(jax.random.fold_in(key, 1), (), 0, RESPS, dtype=jnp.int32)
    return lengths.at[chosen].set(RESPONSE_LENGTH)


def draw_pack_offset(key, part):
    key = jax.random.fold_in(key, 16)
    middle = jax.random.randint(key, (1,), PROMPT_PACK_LEN // 4, 3 * PROMPT_PACK_LEN // 4 + 1, dtype=jnp.int32)
    return jnp.concatenate([jnp.zeros((1,), jnp.int32), middle, jnp.full((1,), PROMPT_PACK_LEN, jnp.int32)])


def place_ends(drawn, rng, smallest, largest):
    extent = drawn.shape
    index_at = [jax.random.randint(jax.random.fold_in(rng, axis), (), 0, extent[axis]) for axis in range(len(extent))]
    drawn = drawn.at[tuple(index_at)].set(smallest)
    longest = extent.index(max(extent))
    index_at[longest] = (index_at[longest] + 1) % extent[longest]
    return drawn.at[tuple(index_at)].set(largest)


def block_levels(stream_key, extent, shards, smallest, high):
    def one(dim, parts):
        draws = jax.random.uniform(jax.random.fold_in(jax.random.fold_in(stream_key, 6), dim), (parts,), jnp.float32, smallest / len(shards), high / len(shards))
        return jnp.repeat(jnp.exp(draws), extent[dim] // parts).reshape((-1,) + (1,) * (len(extent) - dim - 1))

    loudness = one(*shards[0])
    for cut in shards[1:]:
        loudness = loudness * one(*cut)
    return loudness


def scatter_about(rng, shape, scale, most, split=(), kind=jnp.bfloat16):
    result = scale * jax.random.normal(rng, shape, jnp.float32)
    if split:
        result = result * block_levels(rng, shape, split, -0.22, 0.18)
    return jnp.clip(result, -most, most).astype(kind)


def setup_inputs(seed: int = 0) -> dict:
    splits = jax.random.split(jax.random.key(seed), 14)
    resp_query = draw_resp_query(jax.random.fold_in(splits[13], 71), 0)
    resp_key = draw_resp_key(jax.random.fold_in(splits[13], 71), 0)
    resp_value = scatter_about(splits[2], (RESPS, RESPONSE_LENGTH, KEY_VALUE_HEADS * HEAD_SIZE), 1.0, 6.0, ((0, 32), (1, 8)))
    resp_out = scatter_about(splits[3], (RESPS, RESPONSE_LENGTH, HQ * HEAD_SIZE), 0.5, 3.0, ((0, 32), (1, 8)))
    resp_grad = scatter_about(splits[4], (RESPS, RESPONSE_LENGTH, HQ * HEAD_SIZE), 1.0, 6.0, ((0, 32), (1, 8)))
    pack_query = draw_pack_query(jax.random.fold_in(splits[13], 71), 0)
    pack_key = draw_pack_key(jax.random.fold_in(splits[13], 71), 0)
    pack_value = scatter_about(splits[7], (PROMPT_PACK_LEN, KEY_VALUE_HEADS * HEAD_SIZE), 1.0, 6.0, ((0, 256),))
    pack_out = scatter_about(splits[8], (PROMPT_PACK_LEN, HQ * HEAD_SIZE), 0.5, 3.0, ((0, 256),))
    pack_grad = scatter_about(splits[9], (PROMPT_PACK_LEN, HQ * HEAD_SIZE), 1.0, 6.0, ((0, 256),))
    resp_length = draw_resp_length(jax.random.fold_in(splits[13], 71), 0)
    prompt_id = place_ends(jax.random.randint(splits[11], (RESPS,), 0, PROMPTS), jax.random.fold_in(splits[11], 1), 0, PROMPTS - 1).astype(jnp.int32)
    pack_offset = draw_pack_offset(jax.random.fold_in(splits[13], 71), 0)
    return dict(resp_query=resp_query, resp_key=resp_key, resp_value=resp_value, resp_out=resp_out, resp_grad=resp_grad, pack_query=pack_query, pack_key=pack_key, pack_value=pack_value, pack_out=pack_out, pack_grad=pack_grad, resp_length=resp_length, prompt_id=prompt_id, pack_offset=pack_offset)


def attend(queries, cotangent, output, all_keys, all_values, key_mask):
    row_count = queries.shape[0]
    key_count = all_keys.shape[0]
    score_scale = HEAD_SIZE ** -0.5
    query_heads = queries.reshape(row_count, KEY_VALUE_HEADS, HQ // KEY_VALUE_HEADS, HEAD_SIZE).astype(jnp.float32)
    grad_heads = cotangent.reshape(row_count, KEY_VALUE_HEADS, HQ // KEY_VALUE_HEADS, HEAD_SIZE).astype(jnp.float32)
    out_heads = output.reshape(row_count, KEY_VALUE_HEADS, HQ // KEY_VALUE_HEADS, HEAD_SIZE).astype(jnp.float32)
    key_heads = all_keys.reshape(key_count, KEY_VALUE_HEADS, HEAD_SIZE).astype(jnp.float32)
    value_heads = all_values.reshape(key_count, KEY_VALUE_HEADS, HEAD_SIZE).astype(jnp.float32)
    row_delta = jnp.sum(grad_heads * out_heads, axis=-1)
    query_list, key_list, value_list = [], [], []
    for kv_head in range(KEY_VALUE_HEADS):
        scores = jnp.einsum("rgd,jd->grj", query_heads[:, kv_head], key_heads[:, kv_head]) * score_scale
        scores = jnp.where(key_mask[None], scores, -jnp.inf)
        row_top = jnp.max(scores, axis=-1, keepdims=True)
        row_total = jnp.sum(jnp.exp(scores - row_top), axis=-1, keepdims=True)
        softmax_prob = jnp.exp(scores - (row_top + jnp.log(row_total)))
        weights = lax.optimization_barrier(softmax_prob.astype(jnp.bfloat16)).astype(jnp.float32)
        grad_prob = jnp.einsum("rgd,jd->grj", grad_heads[:, kv_head], value_heads[:, kv_head])
        shift_delta = jnp.transpose(row_delta[:, kv_head])[:, :, None]
        dscore = lax.optimization_barrier((softmax_prob * (grad_prob - shift_delta)).astype(jnp.bfloat16)).astype(jnp.float32)
        query_list.append(jnp.einsum("grj,jd->rgd", dscore, key_heads[:, kv_head]) * score_scale)
        key_list.append(jnp.einsum("grj,rgd->jd", dscore, query_heads[:, kv_head]) * score_scale)
        value_list.append(jnp.einsum("grj,rgd->jd", weights, grad_heads[:, kv_head]))
    query_grad = jnp.stack(query_list, axis=1).reshape(row_count, HQ * HEAD_SIZE)
    key_grad = jnp.stack(key_list, axis=1).reshape(key_count, KEY_VALUE_HEADS * HEAD_SIZE)
    value_gradient = jnp.stack(value_list, axis=1).reshape(key_count, KEY_VALUE_HEADS * HEAD_SIZE)
    return query_grad, key_grad, value_gradient


def prompt_of(positions, pack_offset):
    return jnp.sum((positions[:, None] >= pack_offset[None, 1:PROMPTS]).astype(jnp.int32), axis=1)


def reference(resp_query, resp_key, resp_value, resp_out, resp_grad, pack_query, pack_key, pack_value, pack_out, pack_grad, resp_length, prompt_id, pack_offset):
    position = jnp.arange(PROMPT_PACK_LEN, dtype=jnp.int32)
    pack_prompt = prompt_of(position, pack_offset)
    pack_mask = (pack_prompt[:, None] == pack_prompt[None, :]) & (position[None, :] <= position[:, None])
    pack_qgrad, pack_kgrad, pack_vgrad = attend(pack_query, pack_grad, pack_out, pack_key, pack_value, pack_mask)
    steps_resp = jnp.arange(RESPONSE_LENGTH, dtype=jnp.int32)

    def one_response(running_sum, resp_item):
        queries, own_key, own_value, output, cotangent, length, prompt = resp_item
        live_rows = (steps_resp < length)[:, None]
        live_grad = jnp.where(live_rows, cotangent, jnp.zeros_like(cotangent))
        all_keys = jnp.concatenate([pack_key, own_key], axis=0)
        all_values = jnp.concatenate([pack_value, own_value], axis=0)
        prefix_mask = jnp.broadcast_to((pack_prompt == prompt)[None, :], (R_DEV, PROMPT_PACK_LEN))
        prefix_keys, prefix_values = running_sum
        own_key_total = jnp.zeros((RESPONSE_LENGTH, KEY_VALUE_HEADS * HEAD_SIZE), jnp.float32)
        own_value_total = jnp.zeros((RESPONSE_LENGTH, KEY_VALUE_HEADS * HEAD_SIZE), jnp.float32)
        query_parts = []
        for block in range(N_CTX):
            low = block * R_DEV
            high = low + R_DEV
            rows_here = steps_resp[low:high]
            causal = steps_resp[None, :] <= rows_here[:, None]
            key_mask = jnp.concatenate([prefix_mask, causal], axis=1)
            query_grad, key_grad, value_gradient = attend(queries[low:high], live_grad[low:high], output[low:high], all_keys, all_values, key_mask)
            query_parts.append(query_grad.astype(jnp.bfloat16))
            prefix_keys = prefix_keys + key_grad[:PROMPT_PACK_LEN]
            prefix_values = prefix_values + value_gradient[:PROMPT_PACK_LEN]
            own_key_total = own_key_total + lax.optimization_barrier(key_grad[PROMPT_PACK_LEN:].astype(jnp.bfloat16)).astype(jnp.float32)
            own_value_total = own_value_total + lax.optimization_barrier(value_gradient[PROMPT_PACK_LEN:].astype(jnp.bfloat16)).astype(jnp.float32)
        query_combined = jnp.concatenate(query_parts, axis=0)
        return (prefix_keys, prefix_values), (query_combined, own_key_total.astype(jnp.bfloat16), own_value_total.astype(jnp.bfloat16))

    start_sums = (pack_kgrad, pack_vgrad)
    sums_out, resp_grads = lax.scan(one_response, start_sums, (resp_query, resp_key, resp_value, resp_out, resp_grad, resp_length, prompt_id))
    return (resp_grads[0], resp_grads[1], resp_grads[2], pack_qgrad.astype(jnp.bfloat16), sums_out[0].astype(jnp.bfloat16), sums_out[1].astype(jnp.bfloat16))
```

```python
import functools
import math

import jax
import jax.numpy as jnp
from jax import lax
from jax.experimental import pallas as pl
from jax.experimental.pallas import tpu as pltpu
from jax.sharding import PartitionSpec as P

bf, f32 = jnp.bfloat16, jnp.float32
SCALE = 128 ** -0.5
C2 = SCALE * math.log2(math.e)
NEG = -1e30

def dot_t(a, b):
    return lax.dot_general(a, b, (((1,), (1,)), ((), ())), preferred_element_type=f32)
def dot_0(a, b):
    return lax.dot_general(a, b, (((0,), (0,)), ((), ())), preferred_element_type=f32)
def dot(a, b):
    return jnp.dot(a, b, preferred_element_type=f32)

def kernel(CH, DQ, sc_ref, q_ref, g_ref, o_ref, ko_ref, vo_ref, km_ref, vm_ref, kx_ref, vx_ref, pq_ref, pg_ref, po_ref,
           dq_ref, down_ref, dm_ref, dx_ref, pdq_ref,
           bias_ref, pbias_ref, k_ref, v_ref, kt_ref, qs_ref, gs_ref, dl_ref, dk_ref, dv_ref):
    h = pl.program_id(0)
    ctx, core, live, lo, hi, row0, split = [sc_ref[i] for i in range(7)]

    @pl.when(h == 0)
    def _():
        i = lax.broadcasted_iota(jnp.int32, (512, 128), 0)
        half, i = i >> 8, i & 255
        c = (core + half) & 1
        pos = (i >> 5) * 64 + ((i & 31) >> 1) * 4 + c * 2 + (i & 1)
        bias_ref[0:512] = jnp.where((pos >= lo) & (pos < hi), 0.0, NEG)
        u = lax.broadcasted_iota(jnp.int32, (1024, 128), 0)
        r = lax.broadcasted_iota(jnp.int32, (1024, 128), 1)
        bias_ref[512:1536] = jnp.where(u <= ctx * 128 + r, 0.0, NEG)
        prow = row0 + (lax.broadcasted_iota(jnp.int32, (512, 128), 1) & 1)
        seen = (pos <= prow) & ((pos >= split) == (prow >= split))
        pbias_ref[...] = jnp.where(seen, 0.0, NEG)

    k_ref[0:256] = km_ref[...]; k_ref[256:512] = kx_ref[...]; k_ref[512:] = ko_ref[...]
    v_ref[0:256] = vm_ref[...]; v_ref[256:512] = vx_ref[...]; v_ref[512:] = vo_ref[...]
    if DQ == 0:
        kt_ref[...] = k_ref[...].T
    rr = lax.broadcasted_iota(jnp.int32, (128, 128), 0)
    ones = jnp.ones((8, 256), bf)
    for g in range(8):
        s = slice(g * 128, g * 128 + 128)
        qs_ref[s] = q_ref[:, s]
        gg = jnp.where(rr < live, g_ref[:, s].astype(f32), 0.0)
        gs_ref[s] = gg.astype(bf)
        prod = gg * o_ref[:, s].astype(f32)
        ph = prod.astype(bf)
        pl_ = (prod - ph.astype(f32)).astype(bf)
        dl_ref[:, s] = dot_t(ones, jnp.concatenate([ph, pl_], axis=1))
    zero = jnp.zeros((112, 128), f32)
    def rows16(ref):
        x = ref[...].astype(f32)
        return jnp.concatenate([x[:, g * 128:g * 128 + 128] for g in range(8)] + [zero], axis=0)
    pq, pg, po = rows16(pq_ref), rows16(pg_ref), rows16(po_ref)
    prod = pg * po
    ph = prod.astype(bf)
    pl_ = (prod - ph.astype(f32)).astype(bf)
    pdl = dot_t(ones, jnp.concatenate([ph, pl_], axis=1))[0:1]
    pqb, pgb = pq.astype(bf), pg.astype(bf)

    def block(nk, K, V, bias, Q, G, delta):
        S = dot_t(K, Q) + bias
        m = jnp.max(S, axis=0, keepdims=True) * C2
        e = jnp.exp2(S * C2 - m)
        inv = 1.0 / jnp.sum(e, axis=0, keepdims=True)
        p = e * inv
        w = p.astype(bf)
        dP = dot_t(V, G)
        ds = (p * (dP - delta)).astype(bf)
        return w, ds

    w, ds = block(512, k_ref[0:512], v_ref[0:512], pbias_ref[...], pqb, pgb, pdl)
    dv_ref[0:512] = dot(w, pgb)
    dk_ref[0:512] = dot(ds, pqb)
    pdq = (dot_0(ds, k_ref[0:512]) if DQ else dot(kt_ref[:, 0:512], ds).T) * SCALE
    for g in range(8):
        pdq_ref[:, g * 128:g * 128 + 128] = pdq[2 * g:2 * g + 2].astype(bf)
    dv_ref[512:] = jnp.zeros((1024, 128), f32)
    dk_ref[512:] = jnp.zeros((1024, 128), f32)

    def chunk(i):
        rows = pl.ds(i * CH if isinstance(i, int) else pl.multiple_of(i * CH, CH), CH)
        Q, G = qs_ref[rows], gs_ref[rows]
        bias = jnp.concatenate([bias_ref[...]] * (CH // 128), axis=1)
        w, ds = block(1536, k_ref[...], v_ref[...], bias, Q, G, dl_ref[0:1, rows])
        dv_ref[...] += dot(w, G)
        dk_ref[...] += dot(ds, Q)
        dq = (dot_0(ds, k_ref[...]) if DQ else dot(kt_ref[...], ds).T) * SCALE
        for j in range(CH // 128):
            off = i * CH + j * 128
            dq_ref[:, pl.ds(off if isinstance(i, int) else pl.multiple_of(off, 128), 128)] = dq[j * 128:j * 128 + 128].astype(bf)
    pl.loop(0, 1024 // CH)(chunk)
    for dst, sl in ((dm_ref, slice(0, 256)), (dx_ref, slice(256, 512)), (down_ref, slice(512, 1536))):
        dst[:, 0:128] = (dk_ref[sl] * SCALE).astype(bf)
        dst[:, 128:256] = dv_ref[sl].astype(bf)

def attention(sc, q, g, o, kv_own, kv_m, kv_x, pq, pg, po, CH=256, DQ=0):
    wide = lambda n: pl.BlockSpec((n, 1024), lambda h: (0, h))
    kb = lambda n: pl.BlockSpec((n, 128), lambda h: (0, h))
    vb = lambda n: pl.BlockSpec((n, 128), lambda h: (0, 4 + h))
    db = lambda n: pl.BlockSpec((n, 256), lambda h: (0, h))
    return pl.pallas_call(
        functools.partial(kernel, CH, DQ),
        grid=(4,),
        in_specs=[pl.BlockSpec(memory_space=pltpu.SMEM), wide(128), wide(128), wide(128), kb(1024), vb(1024), kb(256), vb(256), kb(256), vb(256),
                  wide(2), wide(2), wide(2)],
        out_specs=[wide(128), db(1024), db(256), db(256), wide(2)],
        out_shape=[jax.ShapeDtypeStruct((128, 4096), bf), jax.ShapeDtypeStruct((1024, 1024), bf), jax.ShapeDtypeStruct((256, 1024), bf),
                   jax.ShapeDtypeStruct((256, 1024), bf), jax.ShapeDtypeStruct((2, 4096), bf)],
        scratch_shapes=[pltpu.VMEM((1536, 128), f32), pltpu.VMEM((512, 128), f32), pltpu.VMEM((1536, 128), bf), pltpu.VMEM((1536, 128), bf),
                        pltpu.VMEM((128, 1536), bf), pltpu.VMEM((1024, 128), bf), pltpu.VMEM((1024, 128), bf), pltpu.VMEM((8, 1024), f32),
                        pltpu.VMEM((1536, 128), f32), pltpu.VMEM((1536, 128), f32)],
        compiler_params=pltpu.CompilerParams(vmem_limit_bytes=48 * 1024 * 1024),
        cost_estimate=pl.CostEstimate(flops=8 * 10**9, bytes_accessed=12 * 2**20, transcendentals=6 * 10**6),
    )(sc, q, g, o, kv_own, kv_own, kv_m, kv_m, kv_x, kv_x, pq, pg, po)


YZ = [[c + 2 * i for i in range(16)] for c in range(2)]
SWAP = [(i, i ^ 1) for i in range(32)]


def halves(total):
    rows = total.shape[0]
    split = total.reshape(rows, 4, 2, 128)
    return split[:, :, 0].reshape(rows, 512), split[:, :, 1].reshape(rows, 512)


def spread(block, axis, count, groups=None):
    copies = jnp.broadcast_to(block[None], (count,) + block.shape)
    got = lax.all_to_all(copies, axis, 0, 0, tiled=True, axis_index_groups=groups)
    return got.reshape((count * block.shape[0],) + block.shape[1:])


def collect(parts, axis, count, groups=None):
    rows = parts.shape[0] // count
    got = lax.all_to_all(parts.reshape((count, rows) + parts.shape[1:]), axis, 0, 0, tiled=True, axis_index_groups=groups)
    return jnp.sum(got.astype(f32), axis=0)


def shards(
    resp_query, resp_key, resp_value, resp_out, resp_grad,
    pack_query, pack_key, pack_value, pack_out, pack_grad,
    resp_length, prompt_id, pack_offset,
):
    ctx = lax.axis_index("ctx")
    resp = lax.axis_index("resp")
    middle = pack_offset[1]
    first = prompt_id[0] == 0
    scalars = jnp.stack([
        ctx, resp & 1, resp_length[0] - ctx * 128,
        jnp.where(first, 0, middle), jnp.where(first, middle, 512),
        (ctx * 32 + resp) * 2, middle,
    ]).astype(jnp.int32)
    own = spread(jnp.concatenate([resp_key[0], resp_value[0]], axis=1), "ctx", 8)
    pack = spread(jnp.concatenate([pack_key, pack_value], axis=1), "resp", 16, YZ)
    mine = spread(pack, "ctx", 8)
    other = lax.ppermute(mine, "resp", SWAP)
    dq, down, dmine, dother, pdq = attention(
        scalars, resp_query[0], resp_grad[0], resp_out[0], own, mine, other, pack_query, pack_grad, pack_out
    )
    own_total = collect(down, "ctx", 8).astype(bf)
    both = (dmine.astype(f32) + lax.ppermute(dother, "resp", SWAP).astype(f32)).astype(bf)
    group = collect(both, "ctx", 8).astype(bf)
    total = collect(group, "resp", 16, YZ).astype(bf)
    own_key, own_value = halves(own_total)
    block_key, block_value = halves(total)
    return dq[None], own_key[None], own_value[None], pdq, block_key, block_value


def solution(mesh):
    long = P("resp", "ctx", None)
    pack = P(("ctx", "resp"), None)
    return jax.shard_map(
        shards,
        mesh=mesh,
        in_specs=(long,) * 5 + (pack,) * 5 + (P("resp"), P("resp"), P()),
        out_specs=(long,) * 3 + (pack,) * 3,
        check_vma=False,
    )
```

```python
import functools
import math

import jax
import jax.numpy as jnp
from jax import lax
from jax.experimental import pallas as pl
from jax.experimental.pallas import tpu as pltpu
from jax.sharding import PartitionSpec as P

bf, f32 = jnp.bfloat16, jnp.float32
SCALE = 128 ** -0.5
C2 = SCALE * math.log2(math.e)
NEG = -1e30

def dot_t(a, b):
    return lax.dot_general(a, b, (((1,), (1,)), ((), ())), preferred_element_type=f32)
def dot_0(a, b):
    return lax.dot_general(a, b, (((0,), (0,)), ((), ())), preferred_element_type=f32)
def dot(a, b):
    return jnp.dot(a, b, preferred_element_type=f32)

def kernel(CH, DQ, sc_ref, q_ref, g_ref, o_ref, ko_ref, vo_ref, km_ref, vm_ref, kx_ref, vx_ref, pq_ref, pg_ref, po_ref,
           dq_ref, down_ref, dm_ref, dx_ref, pdq_ref,
           bias_ref, pbias_ref, k_ref, v_ref, kt_ref, qs_ref, gs_ref, dl_ref, dk_ref, dv_ref):
    h = pl.program_id(0)
    ctx, core, live, lo, hi, row0, split = [sc_ref[i] for i in range(7)]

    @pl.when(h == 0)
    def _():
        i = lax.broadcasted_iota(jnp.int32, (512, 128), 0)
        half, i = i >> 8, i & 255
        pos = (((i >> 1) << 2) | (half << 1) | (i & 1)) ^ row0
        bias_ref[0:512] = jnp.where((pos >= lo) & (pos < hi), 0.0, NEG)
        u = lax.broadcasted_iota(jnp.int32, (1024, 128), 0)
        r = lax.broadcasted_iota(jnp.int32, (1024, 128), 1)
        bias_ref[512:1536] = jnp.where(u <= ctx * 128 + r, 0.0, NEG)
        prow = row0 + (lax.broadcasted_iota(jnp.int32, (512, 128), 1) & 1)
        seen = (pos <= prow) & ((pos >= split) == (prow >= split))
        pbias_ref[...] = jnp.where(seen, 0.0, NEG)

    k_ref[0:256] = km_ref[...]; k_ref[256:512] = kx_ref[...]; k_ref[512:] = ko_ref[...]
    v_ref[0:256] = vm_ref[...]; v_ref[256:512] = vx_ref[...]; v_ref[512:] = vo_ref[...]
    if DQ == 0:
        kt_ref[...] = k_ref[...].T
    rr = lax.broadcasted_iota(jnp.int32, (128, 128), 0)
    ones = jnp.ones((8, 256), bf)
    for g in range(8):
        s = slice(g * 128, g * 128 + 128)
        qs_ref[s] = q_ref[:, s]
        gg = jnp.where(rr < live, g_ref[:, s].astype(f32), 0.0)
        gs_ref[s] = gg.astype(bf)
        prod = gg * o_ref[:, s].astype(f32)
        ph = prod.astype(bf)
        pl_ = (prod - ph.astype(f32)).astype(bf)
        dl_ref[:, s] = dot_t(ones, jnp.concatenate([ph, pl_], axis=1))
    zero = jnp.zeros((112, 128), f32)
    def rows16(ref):
        x = ref[...].astype(f32)
        return jnp.concatenate([x[:, g * 128:g * 128 + 128] for g in range(8)] + [zero], axis=0)
    pq, pg, po = rows16(pq_ref), rows16(pg_ref), rows16(po_ref)
    prod = pg * po
    ph = prod.astype(bf)
    pl_ = (prod - ph.astype(f32)).astype(bf)
    pdl = dot_t(ones, jnp.concatenate([ph, pl_], axis=1))[0:1]
    pqb, pgb = pq.astype(bf), pg.astype(bf)

    def block(nk, K, V, bias, Q, G, delta):
        S = dot_t(K, Q) + bias
        m = jnp.max(S, axis=0, keepdims=True) * C2
        e = jnp.exp2(S * C2 - m)
        inv = 1.0 / jnp.sum(e, axis=0, keepdims=True)
        p = e * inv
        w = p.astype(bf)
        dP = dot_t(V, G)
        ds = (p * (dP - delta)).astype(bf)
        return w, ds

    w, ds = block(512, k_ref[0:512], v_ref[0:512], pbias_ref[...], pqb, pgb, pdl)
    dv_ref[0:512] = dot(w, pgb)
    dk_ref[0:512] = dot(ds, pqb)
    pdq = (dot_0(ds, k_ref[0:512]) if DQ else dot(kt_ref[:, 0:512], ds).T) * SCALE
    for g in range(8):
        pdq_ref[:, g * 128:g * 128 + 128] = pdq[2 * g:2 * g + 2].astype(bf)
    dv_ref[512:] = jnp.zeros((1024, 128), f32)
    dk_ref[512:] = jnp.zeros((1024, 128), f32)

    def chunk(i):
        rows = pl.ds(i * CH if isinstance(i, int) else pl.multiple_of(i * CH, CH), CH)
        Q, G = qs_ref[rows], gs_ref[rows]
        bias = jnp.concatenate([bias_ref[...]] * (CH // 128), axis=1)
        w, ds = block(1536, k_ref[...], v_ref[...], bias, Q, G, dl_ref[0:1, rows])
        dv_ref[...] += dot(w, G)
        dk_ref[...] += dot(ds, Q)
        dq = (dot_0(ds, k_ref[...]) if DQ else dot(kt_ref[...], ds).T) * SCALE
        for j in range(CH // 128):
            off = i * CH + j * 128
            dq_ref[:, pl.ds(off if isinstance(i, int) else pl.multiple_of(off, 128), 128)] = dq[j * 128:j * 128 + 128].astype(bf)
    pl.loop(0, 1024 // CH)(chunk)
    for dst, sl in ((dm_ref, slice(0, 256)), (dx_ref, slice(256, 512)), (down_ref, slice(512, 1536))):
        dst[:, 0:128] = (dk_ref[sl] * SCALE).astype(bf)
        dst[:, 128:256] = dv_ref[sl].astype(bf)

def attention(sc, q, g, o, kv_own, kv_m, kv_x, pq, pg, po, CH=512, DQ=0):
    wide = lambda n: pl.BlockSpec((n, 1024), lambda h: (0, h))
    kb = lambda n: pl.BlockSpec((n, 128), lambda h: (0, h))
    vb = lambda n: pl.BlockSpec((n, 128), lambda h: (0, 4 + h))
    db = lambda n: pl.BlockSpec((n, 256), lambda h: (0, h))
    return pl.pallas_call(
        functools.partial(kernel, CH, DQ),
        grid=(4,),
        in_specs=[pl.BlockSpec(memory_space=pltpu.SMEM), wide(128), wide(128), wide(128), kb(1024), vb(1024), kb(256), vb(256), kb(256), vb(256),
                  wide(2), wide(2), wide(2)],
        out_specs=[wide(128), db(1024), db(256), db(256), wide(2)],
        out_shape=[jax.ShapeDtypeStruct((128, 4096), bf), jax.ShapeDtypeStruct((1024, 1024), bf), jax.ShapeDtypeStruct((256, 1024), bf),
                   jax.ShapeDtypeStruct((256, 1024), bf), jax.ShapeDtypeStruct((2, 4096), bf)],
        scratch_shapes=[pltpu.VMEM((1536, 128), f32), pltpu.VMEM((512, 128), f32), pltpu.VMEM((1536, 128), bf), pltpu.VMEM((1536, 128), bf),
                        pltpu.VMEM((128, 1536), bf), pltpu.VMEM((1024, 128), bf), pltpu.VMEM((1024, 128), bf), pltpu.VMEM((8, 1024), f32),
                        pltpu.VMEM((1536, 128), f32), pltpu.VMEM((1536, 128), f32)],
        compiler_params=pltpu.CompilerParams(vmem_limit_bytes=48 * 1024 * 1024),
        cost_estimate=pl.CostEstimate(flops=8 * 10**9, bytes_accessed=12 * 2**20, transcendentals=6 * 10**6),
    )(sc, q, g, o, kv_own, kv_own, kv_m, kv_m, kv_x, kv_x, pq, pg, po)


def partners(mask, size):
    return [(i, i ^ mask) for i in range(size)]


def swap(block, axis, mask):
    return lax.ppermute(block, axis, partners(mask, 8 if axis == "ctx" else 32))


def copies_kernel(key_ref, value_ref, out_ref):
    for i in range(8):
        out_ref[i, :, 0:512] = key_ref[...]
        out_ref[i, :, 512:1024] = value_ref[...]


def copies_of(key, value):
    return pl.pallas_call(
        copies_kernel,
        out_shape=jax.ShapeDtypeStruct((8, 128, 1024), bf),
        cost_estimate=pl.CostEstimate(flops=0, bytes_accessed=2**21, transcendentals=0),
    )(key, value)


def join_kernel(*refs):
    refs[-1][...] = jnp.concatenate([ref[...].astype(f32) for ref in refs[:-1]], axis=0).astype(bf)


def join(*blocks):
    rows, width = blocks[0].shape
    return pl.pallas_call(
        join_kernel,
        out_shape=jax.ShapeDtypeStruct((len(blocks) * rows, width), bf),
        cost_estimate=pl.CostEstimate(flops=0, bytes_accessed=len(blocks) * rows * width * 4, transcendentals=0),
    )(*blocks)


def widen_kernel(key_ref, value_ref, out_ref):
    both = jnp.concatenate([key_ref[...].astype(f32), value_ref[...].astype(f32)], axis=1)
    out_ref[...] = both.astype(bf)


def widen(key, value):
    return pl.pallas_call(
        widen_kernel, out_shape=jax.ShapeDtypeStruct((key.shape[0], 1024), bf)
    )(key, value)


def fold_kernel(count, *refs):
    total = refs[0][...].astype(f32)
    for ref in refs[1:count]:
        total = total + ref[...].astype(f32)
    rows = total.shape[0] // (len(refs) - count)
    for i, ref in enumerate(refs[count:]):
        ref[...] = total[i * rows : i * rows + rows].astype(bf)


def fold(blocks, ways):
    rows, width = blocks[0].shape
    return pl.pallas_call(
        functools.partial(fold_kernel, len(blocks)),
        out_shape=[jax.ShapeDtypeStruct((rows // ways, width), bf)] * ways,
        cost_estimate=pl.CostEstimate(flops=0, bytes_accessed=len(blocks) * rows * width * 4, transcendentals=0),
    )(*blocks)


def finish_kernel(count, *refs):
    if count == 1:
        total = jnp.sum(refs[0][...].astype(f32), axis=0)
    else:
        total = refs[0][...].astype(f32)
        for ref in refs[1:count]:
            total = total + ref[...].astype(f32)
    for h in range(4):
        refs[count][:, h * 128 : h * 128 + 128] = total[:, h * 256 : h * 256 + 128].astype(bf)
        refs[count + 1][:, h * 128 : h * 128 + 128] = total[:, h * 256 + 128 : h * 256 + 256].astype(bf)


def finish(*blocks):
    rows = blocks[0].shape[-2]
    return pl.pallas_call(
        functools.partial(finish_kernel, len(blocks)),
        out_shape=[jax.ShapeDtypeStruct((rows, 512), bf)] * 2,
    )(*blocks)


def shards(
    resp_query, resp_key, resp_value, resp_out, resp_grad,
    pack_query, pack_key, pack_value, pack_out, pack_grad,
    resp_length, prompt_id, pack_offset,
):
    ctx = lax.axis_index("ctx")
    resp = lax.axis_index("resp")
    middle = pack_offset[1]
    first = prompt_id[0] == 0
    scalars = jnp.stack([
        ctx, resp & 1, resp_length[0] - ctx * 128,
        jnp.where(first, 0, middle), jnp.where(first, middle, 512),
        (ctx * 32 + resp) * 2, middle,
    ]).astype(jnp.int32)
    copies = copies_of(resp_key[0], resp_value[0])
    block, copies = lax.optimization_barrier((widen(pack_key, pack_value), copies))
    own = lax.all_to_all(copies, "ctx", 0, 0, tiled=True).reshape(1024, 1024)
    block = join(block, *[swap(block, "resp", m) for m in (2, 4, 6)])
    block = join(block, *[swap(block, "resp", m) for m in (8, 16, 24)])
    block = join(block, *[swap(block, "ctx", m) for m in (1, 2, 3)])
    mine = join(block, swap(block, "ctx", 4))
    other = swap(mine, "resp", 1)
    dq, down, dmine, dother, pdq = attention(
        scalars, resp_query[0], resp_grad[0], resp_out[0], own, mine, other, pack_query, pack_grad, pack_out
    )
    own_parts = lax.all_to_all(down.reshape(8, 128, 1024), "ctx", 0, 0, tiled=True)
    keep, away = fold([dmine, swap(dother, "resp", 1)], 2)
    parts = fold([keep, swap(away, "ctx", 4)], 4)
    parts = fold([parts[0]] + [swap(parts[m], "ctx", m) for m in (1, 2, 3)], 4)
    parts = fold([parts[0]] + [swap(parts[m], "resp", 8 * m) for m in (1, 2, 3)], 4)
    block_key, block_value = finish(parts[0], *[swap(parts[m], "resp", 2 * m) for m in (1, 2, 3)])
    own_key, own_value = finish(own_parts)
    return dq[None], own_key[None], own_value[None], pdq, block_key, block_value


def solution(mesh):
    long = P("resp", "ctx", None)
    pack = P(("ctx", "resp"), None)
    return jax.shard_map(
        shards,
        mesh=mesh,
        in_specs=(long,) * 5 + (pack,) * 5 + (P("resp"), P("resp"), P()),
        out_specs=(long,) * 3 + (pack,) * 3,
        check_vma=False,
    )
```

```python
import functools
import math

import jax
import jax.numpy as jnp
from jax import lax
from jax.experimental import pallas as pl
from jax.experimental.pallas import tpu as pltpu
from jax.sharding import PartitionSpec as P

bf, f32 = jnp.bfloat16, jnp.float32
SCALE = 128 ** -0.5
C2 = SCALE * math.log2(math.e)
NEG = -1e30
LIMIT = pltpu.CompilerParams(vmem_limit_bytes=60 * 1024 * 1024)
SMALL = pltpu.CompilerParams(vmem_limit_bytes=12 * 1024 * 1024)


def dot_t(a, b):
    return lax.dot_general(a, b, (((1,), (1,)), ((), ())), preferred_element_type=f32)


def dot(a, b):
    return jnp.dot(a, b, preferred_element_type=f32)


def row_delta(grad, out):
    prod = grad * out
    high = prod.astype(bf)
    low = (prod - high.astype(f32)).astype(bf)
    return dot_t(jnp.ones((8, 256), bf), jnp.concatenate([high, low], axis=1))


def causal_bias(ctx):
    u = lax.broadcasted_iota(jnp.int32, (1024, 128), 0)
    r = lax.broadcasted_iota(jnp.int32, (1024, 128), 1)
    return jnp.where(u <= ctx * 128 + r, 0.0, NEG)


def own_stats_kernel(CH, len_ref, q_ref, g_ref, o_ref, k_ref, qs_ref, gs_ref, st_ref, bias_ref):
    @pl.when(pl.program_id(0) == 0)
    def _():
        bias_ref[...] = causal_bias(lax.axis_index("ctx"))

    live = len_ref[0] - lax.axis_index("ctx") * 128
    rr = lax.broadcasted_iota(jnp.int32, (128, 128), 0)
    for g in range(8):
        s = slice(g * 128, g * 128 + 128)
        qs_ref[0, s] = q_ref[:, s]
        grad = jnp.where(rr < live, g_ref[:, s].astype(f32), 0.0)
        gs_ref[0, s] = grad.astype(bf)
        st_ref[0, 16:24, s] = row_delta(grad, o_ref[:, s].astype(f32))

    K = k_ref[...].reshape(1024, 128)

    @pl.loop(0, 1024 // CH)
    def _(i):
        rows = pl.ds(pl.multiple_of(i * CH, CH), CH)
        S = dot_t(K, qs_ref[0, rows]) + jnp.concatenate([bias_ref[...]] * (CH // 128), axis=1)
        m = jnp.max(S, axis=0, keepdims=True) * C2
        total = jnp.sum(jnp.exp2(S * C2 - m), axis=0, keepdims=True)
        st_ref[0, 0:8, rows] = jnp.broadcast_to(m, (8, CH))
        st_ref[0, 8:16, rows] = jnp.broadcast_to(total, (8, CH))


def prefix_kernel(CH, prompt_ref, offset_ref, qs_ref, gs_ref, st_ref, km_ref, vm_ref, kx_ref, vx_ref, pq_ref, pg_ref, po_ref,
                  dm_ref, dx_ref, dqt_ref, lse_ref, pdq_ref, bias_ref, pbias_ref, k_ref, v_ref, dk_ref, dv_ref):
    resp = lax.axis_index("resp")
    core, row0 = resp & 1, (lax.axis_index("ctx") * 32 + resp) * 2
    split = offset_ref[1]
    lo = jnp.where(prompt_ref[0] == 0, 0, split)
    hi = jnp.where(prompt_ref[0] == 0, split, 512)

    @pl.when(pl.program_id(0) == 0)
    def _():
        i = lax.broadcasted_iota(jnp.int32, (512, 128), 0)
        side, j = i >> 8, i & 255
        pos = (j >> 5) * 64 + ((resp >> 1) ^ ((j >> 1) & 15)) * 4 + (core ^ side) * 2 + (j & 1)
        bias_ref[...] = jnp.where((pos >= lo) & (pos < hi), 0.0, NEG)
        prow = row0 + (lax.broadcasted_iota(jnp.int32, (512, 128), 1) & 1)
        seen = (pos <= prow) & ((pos >= split) == (prow >= split))
        pbias_ref[...] = jnp.where(seen, 0.0, NEG)

    k_ref[0:256] = km_ref[...].reshape(256, 128)
    k_ref[256:512] = kx_ref[...].reshape(256, 128)
    v_ref[0:256] = vm_ref[...].reshape(256, 128)
    v_ref[256:512] = vx_ref[...].reshape(256, 128)
    K, V = k_ref[...], v_ref[...]
    KT = K.T

    zero = jnp.zeros((112, 128), f32)

    def rows16(ref):
        x = ref[...].astype(f32)
        return jnp.concatenate([x[:, g * 128 : g * 128 + 128] for g in range(8)] + [zero], axis=0)

    pq, pg, po = rows16(pq_ref), rows16(pg_ref), rows16(po_ref)
    delta = row_delta(pg, po)[0:1]
    pq, pg = pq.astype(bf), pg.astype(bf)
    S = dot_t(K, pq) + pbias_ref[...]
    m = jnp.max(S, axis=0, keepdims=True) * C2
    e = jnp.exp2(S * C2 - m)
    p = e * (1.0 / jnp.sum(e, axis=0, keepdims=True))
    ds = (p * (dot_t(V, pg) - delta)).astype(bf)
    dv_ref[...] = dot(p.astype(bf), pg)
    dk_ref[...] = dot(ds, pq)
    pdq = dot(KT, ds).T * SCALE
    for g in range(8):
        pdq_ref[:, g * 128 : g * 128 + 128] = pdq[2 * g : 2 * g + 2].astype(bf)

    @pl.loop(0, 1024 // CH)
    def _(i):
        rows = pl.ds(pl.multiple_of(i * CH, CH), CH)
        Q, G = qs_ref[0, rows], gs_ref[0, rows]
        m_own, l_own, delta = st_ref[0, 0:1, rows], st_ref[0, 8:9, rows], st_ref[0, 16:17, rows]
        S = dot_t(K, Q) + jnp.concatenate([bias_ref[...]] * (CH // 128), axis=1)
        m = jnp.maximum(jnp.max(S, axis=0, keepdims=True) * C2, m_own)
        e = jnp.exp2(S * C2 - m)
        total = jnp.sum(e, axis=0, keepdims=True) + l_own * jnp.exp2(m_own - m)
        lse_ref[0, :, rows] = jnp.broadcast_to(m + jnp.log2(total), (8, CH))
        p = e * (1.0 / total)
        ds = (p * (dot_t(V, G) - delta)).astype(bf)
        dv_ref[...] += dot(p.astype(bf), G)
        dk_ref[...] += dot(ds, Q)
        dqt_ref[0, :, rows] = dot(KT, ds)

    for dst, s in ((dm_ref, slice(0, 256)), (dx_ref, slice(256, 512))):
        dst[:, 0] = (dk_ref[s] * SCALE).astype(bf).reshape(8, 32, 128)
        dst[:, 1] = dv_ref[s].astype(bf).reshape(8, 32, 128)


def own_grads_kernel(CH, qs_ref, gs_ref, st_ref, lse_ref, dqt_ref, k_ref, v_ref, dq_ref, d_ref, bias_ref, dk_ref, dv_ref):
    @pl.when(pl.program_id(0) == 0)
    def _():
        bias_ref[...] = causal_bias(lax.axis_index("ctx"))

    K, V = k_ref[...].reshape(1024, 128), v_ref[...].reshape(1024, 128)
    KT = K.T
    dk_ref[...] = jnp.zeros((1024, 128), f32)
    dv_ref[...] = jnp.zeros((1024, 128), f32)

    @pl.loop(0, 1024 // CH)
    def _(i):
        rows = pl.ds(pl.multiple_of(i * CH, CH), CH)
        Q, G = qs_ref[0, rows], gs_ref[0, rows]
        S = dot_t(K, Q) + jnp.concatenate([bias_ref[...]] * (CH // 128), axis=1)
        p = jnp.exp2(S * C2 - lse_ref[0, 0:1, rows])
        ds = (p * (dot_t(V, G) - st_ref[0, 16:17, rows])).astype(bf)
        dv_ref[...] += dot(p.astype(bf), G)
        dk_ref[...] += dot(ds, Q)
        dq = ((dqt_ref[0, :, rows] + dot(KT, ds)) * SCALE).T
        for j in range(CH // 128):
            lanes = pl.ds(pl.multiple_of(i * CH + j * 128, 128), 128)
            dq_ref[:, lanes] = dq[j * 128 : j * 128 + 128].astype(bf)

    d_ref[:, 0:128] = (dk_ref[...] * SCALE).astype(bf).reshape(8, 128, 128)
    d_ref[:, 128:256] = dv_ref[...].astype(bf).reshape(8, 128, 128)


SMEM = pl.BlockSpec(memory_space=pltpu.SMEM)


def wide(n):
    return pl.BlockSpec((n, 1024), lambda h: (0, h))


def per_head(*shape):
    return pl.BlockSpec((1,) + shape, lambda h: (h, 0, 0))


def own_block(kv):
    return pl.BlockSpec((8, 128, 128), lambda h: (0, 2 * h + kv, 0))


def pack_block(kv):
    return pl.BlockSpec((8, 1, 32, 128), lambda h: (0, 2 * h + kv, 0, 0))


def shape_of(*shape, dtype=bf):
    return jax.ShapeDtypeStruct(shape, dtype)


def cost(gflops, megabytes):
    return pl.CostEstimate(flops=int(gflops * 1e9), bytes_accessed=int(megabytes * 2**20), transcendentals=0)


def own_stats(length, q, g, o, own, CH=1024):
    return pl.pallas_call(
        functools.partial(own_stats_kernel, CH),
        grid=(4,),
        in_specs=[SMEM, wide(128), wide(128), wide(128), own_block(0)],
        out_specs=[per_head(1024, 128), per_head(1024, 128), per_head(24, 1024)],
        out_shape=[shape_of(4, 1024, 128), shape_of(4, 1024, 128), shape_of(4, 24, 1024, dtype=f32)],
        scratch_shapes=[pltpu.VMEM((1024, 128), f32)],
        compiler_params=LIMIT,
        cost_estimate=cost(1.2, 6),
    )(length, q, g, o, own)


def prefix(prompt, offset, qs, gs, st, mine, other, pq, pg, po, CH=1024):
    big = pl.BlockSpec((8, 2, 32, 128), lambda h: (0, h, 0, 0))
    return pl.pallas_call(
        functools.partial(prefix_kernel, CH),
        grid=(4,),
        in_specs=[SMEM, SMEM, per_head(1024, 128), per_head(1024, 128), per_head(24, 1024),
                  pack_block(0), pack_block(1), pack_block(0), pack_block(1), wide(2), wide(2), wide(2)],
        out_specs=[big, big, per_head(128, 1024), per_head(8, 1024), wide(2)],
        out_shape=[shape_of(8, 8, 32, 128), shape_of(8, 8, 32, 128), shape_of(4, 128, 1024, dtype=f32),
                   shape_of(4, 8, 1024, dtype=f32), shape_of(2, 4096)],
        scratch_shapes=[pltpu.VMEM((512, 128), f32), pltpu.VMEM((512, 128), f32), pltpu.VMEM((512, 128), bf),
                        pltpu.VMEM((512, 128), bf), pltpu.VMEM((512, 128), f32), pltpu.VMEM((512, 128), f32)],
        compiler_params=LIMIT,
        cost_estimate=cost(2.7, 8),
    )(prompt, offset, qs, gs, st, mine, mine, other, other, pq, pg, po)


def own_grads(qs, gs, st, lse, dqt, own, CH=1024):
    return pl.pallas_call(
        functools.partial(own_grads_kernel, CH),
        grid=(4,),
        in_specs=[per_head(1024, 128), per_head(1024, 128), per_head(24, 1024), per_head(8, 1024), per_head(128, 1024),
                  own_block(0), own_block(1)],
        out_specs=[wide(128), pl.BlockSpec((8, 256, 128), lambda h: (0, h, 0))],
        out_shape=[shape_of(128, 4096), shape_of(8, 1024, 128)],
        scratch_shapes=[pltpu.VMEM((1024, 128), f32)] * 3,
        compiler_params=LIMIT,
        cost_estimate=cost(5.4, 10),
    )(qs, gs, st, lse, dqt, own, own)


def copies_kernel(key_ref, value_ref, pack_key_ref, pack_value_ref, out_ref, pack_ref, block, sems):
    for h in range(4):
        lanes = slice(h * 128, h * 128 + 128)
        block[h * 256 : h * 256 + 128] = key_ref[:, lanes]
        block[h * 256 + 128 : h * 256 + 256] = value_ref[:, lanes]
    sent = [pltpu.make_async_copy(block, out_ref.at[i], sems.at[i]) for i in range(8)]
    for copy in sent:
        copy.start()
    key, value = pack_key_ref[...].astype(f32), pack_value_ref[...].astype(f32)
    parts = [x[:, h * 128 : h * 128 + 128] for h in range(4) for x in (key, value)]
    pack_ref[...] = jnp.concatenate(parts, axis=0).astype(bf)
    for copy in sent:
        copy.wait()


def copies_of(key, value, pack_key, pack_value):
    return pl.pallas_call(
        copies_kernel,
        out_specs=[pl.BlockSpec(memory_space=pl.ANY), pl.BlockSpec(memory_space=pltpu.VMEM)],
        out_shape=[shape_of(8, 1024, 128), shape_of(16, 128)],
        scratch_shapes=[pltpu.VMEM((1024, 128), bf), pltpu.SemaphoreType.DMA((8,))],
        compiler_params=SMALL,
        cost_estimate=cost(0, 2),
    )(key, value, pack_key, pack_value)


def regroup_kernel(*refs):
    x = jnp.concatenate([ref[...].astype(f32) for ref in refs[:4]], axis=0)
    for k in range(8):
        rows = [x[16 * i + 2 * k : 16 * i + 2 * k + 2] for i in range(16)]
        rows = jnp.concatenate(rows, axis=0).astype(bf)
        for c in range(8):
            refs[4][c, k] = rows


def regroup(*blocks):
    return pl.pallas_call(
        regroup_kernel,
        out_shape=shape_of(8, 8, 32, 128),
        compiler_params=SMALL,
        cost_estimate=cost(0, 1),
    )(*blocks)


def ungroup_kernel(parts_ref, *refs):
    total = jnp.sum(parts_ref[...].astype(f32), axis=0)
    for m in range(4):
        rows = [total[k, 8 * m + 2 * i : 8 * m + 2 * i + 2] for i in range(4) for k in range(8)]
        refs[m][...] = jnp.concatenate(rows, axis=0).astype(bf)


def ungroup(parts):
    return pl.pallas_call(
        ungroup_kernel,
        out_shape=[shape_of(64, 128)] * 4,
        compiler_params=SMALL,
        cost_estimate=cost(0, 1),
    )(parts)


def quarter_kernel(*refs):
    total = sum(ref[...].astype(f32) for ref in refs[:4])
    for m in range(4):
        refs[4 + m][...] = total[16 * m : 16 * m + 16].astype(bf)


def quarter(*blocks):
    return pl.pallas_call(
        quarter_kernel,
        out_shape=[shape_of(16, 128)] * 4,
        compiler_params=SMALL,
        cost_estimate=cost(0, 0.1),
    )(*blocks)


def finish_pack_kernel(a_ref, b_ref, c_ref, d_ref, key_ref, value_ref):
    rows = sum(ref[...].astype(f32) for ref in (a_ref, b_ref, c_ref, d_ref))
    key_ref[...] = jnp.concatenate([rows[4 * h : 4 * h + 2] for h in range(4)], axis=1).astype(bf)
    value_ref[...] = jnp.concatenate([rows[4 * h + 2 : 4 * h + 4] for h in range(4)], axis=1).astype(bf)


def finish_pack(*blocks):
    return pl.pallas_call(finish_pack_kernel, out_shape=[shape_of(2, 512)] * 2, compiler_params=SMALL, cost_estimate=cost(0, 0.1))(*blocks)


def finish_own_kernel(parts_ref, key_ref, value_ref):
    total = jnp.sum(parts_ref[...].astype(f32), axis=0)
    key_ref[...] = total[0:128].astype(bf)
    value_ref[...] = total[128:256].astype(bf)


def finish_own(parts):
    column = pl.BlockSpec((128, 128), lambda h: (0, h))
    return pl.pallas_call(
        finish_own_kernel,
        grid=(4,),
        in_specs=[pl.BlockSpec((8, 256, 128), lambda h: (0, h, 0))],
        out_specs=[column, column],
        out_shape=[shape_of(128, 512), shape_of(128, 512)],
        compiler_params=SMALL,
        cost_estimate=cost(0, 3),
    )(parts)


def from_partner(block, mask):
    return lax.ppermute(block, "resp", [(i, i ^ mask) for i in range(32)])


def exchange(blocks):
    return lax.all_to_all(blocks, "ctx", 0, 0, tiled=True)


def shards(
    resp_query, resp_key, resp_value, resp_out, resp_grad,
    pack_query, pack_key, pack_value, pack_out, pack_grad,
    resp_length, prompt_id, pack_offset,
):
    copies, block = copies_of(resp_key[0], resp_value[0], pack_key, pack_value)
    own = exchange(copies)
    block = jnp.concatenate([block] + [from_partner(block, m) for m in (2, 4, 6)], axis=0)
    mine = exchange(regroup(block, *[from_partner(block, m) for m in (8, 16, 24)]))
    qs, gs, st = own_stats(resp_length, resp_query[0], resp_grad[0], resp_out[0], own)
    mine, st = lax.optimization_barrier((mine, st))
    other = from_partner(mine, 1)
    dmine, dother, dqt, lse, pdq = prefix(
        prompt_id, pack_offset, qs, gs, st, mine, other, pack_query, pack_grad, pack_out
    )
    both = dmine.astype(f32) + from_partner(dother, 1).astype(f32)
    parts = exchange(both.astype(bf))
    dq, down = own_grads(qs, gs, st, lse, dqt, own)
    parts = ungroup(parts)
    own_parts = exchange(down)
    parts = quarter(parts[0], *[from_partner(parts[m], 8 * m) for m in (1, 2, 3)])
    block_key, block_value = finish_pack(parts[0], *[from_partner(parts[m], 2 * m) for m in (1, 2, 3)])
    key, value = finish_own(own_parts)
    return dq[None], key[None], value[None], pdq, block_key, block_value


def solution(mesh):
    long = P("resp", "ctx", None)
    pack = P(("ctx", "resp"), None)
    return jax.shard_map(
        shards,
        mesh=mesh,
        in_specs=(long,) * 5 + (pack,) * 5 + (P("resp"), P("resp"), P()),
        out_specs=(long,) * 3 + (pack,) * 3,
        check_vma=False,
    )
```

```python
import functools
import math

import jax
import jax.numpy as jnp
from jax import lax
from jax.experimental import pallas as pl
from jax.experimental.pallas import tpu as pltpu
from jax.sharding import PartitionSpec as P

bf, f32 = jnp.bfloat16, jnp.float32
SCALE = 128 ** -0.5
C2 = SCALE * math.log2(math.e)
NEG = -1e30
LIMIT = pltpu.CompilerParams(vmem_limit_bytes=60 * 1024 * 1024)
SMALL = pltpu.CompilerParams(vmem_limit_bytes=12 * 1024 * 1024)


def dot_t(a, b):
    return lax.dot_general(a, b, (((1,), (1,)), ((), ())), preferred_element_type=f32)


def dot(a, b):
    return jnp.dot(a, b, preferred_element_type=f32)


def row_delta(grad, out):
    prod = grad * out
    high = prod.astype(bf)
    low = (prod - high.astype(f32)).astype(bf)
    return dot_t(jnp.ones((8, 256), bf), jnp.concatenate([high, low], axis=1))


def causal_bias(ctx):
    u = lax.broadcasted_iota(jnp.int32, (1024, 128), 0)
    r = lax.broadcasted_iota(jnp.int32, (1024, 128), 1)
    return jnp.where(u <= ctx * 128 + r, 0.0, NEG)


def own_stats_kernel(CH, len_ref, q_ref, g_ref, o_ref, k_ref, qs_ref, gs_ref, st_ref, bias_ref):
    @pl.when(pl.program_id(0) == 0)
    def _():
        bias_ref[...] = causal_bias(lax.axis_index("ctx"))

    live = len_ref[0] - lax.axis_index("ctx") * 128
    rr = lax.broadcasted_iota(jnp.int32, (128, 128), 0)
    for g in range(8):
        s = slice(g * 128, g * 128 + 128)
        qs_ref[0, s] = q_ref[:, s]
        grad = jnp.where(rr < live, g_ref[:, s].astype(f32), 0.0)
        gs_ref[0, s] = grad.astype(bf)
        st_ref[0, 16:24, s] = row_delta(grad, o_ref[:, s].astype(f32))

    K = k_ref[...].reshape(1024, 128)

    @pl.loop(0, 1024 // CH)
    def _(i):
        rows = pl.ds(pl.multiple_of(i * CH, CH), CH)
        S = dot_t(K, qs_ref[0, rows]) + jnp.concatenate([bias_ref[...]] * (CH // 128), axis=1)
        m = jnp.max(S, axis=0, keepdims=True) * C2
        total = jnp.sum(jnp.exp2(S * C2 - m), axis=0, keepdims=True)
        st_ref[0, 0:8, rows] = jnp.broadcast_to(m, (8, CH))
        st_ref[0, 8:16, rows] = jnp.broadcast_to(total, (8, CH))


def prefix_kernel(CH, prompt_ref, offset_ref, qs_ref, gs_ref, st_ref, km_ref, vm_ref, kx_ref, vx_ref, pq_ref, pg_ref, po_ref,
                  dm_ref, dx_ref, dqt_ref, lse_ref, pdq_ref, bias_ref, pbias_ref, k_ref, v_ref, dk_ref, dv_ref):
    resp = lax.axis_index("resp")
    core, row0 = resp & 1, (lax.axis_index("ctx") * 32 + resp) * 2
    split = offset_ref[1]
    lo = jnp.where(prompt_ref[0] == 0, 0, split)
    hi = jnp.where(prompt_ref[0] == 0, split, 512)

    @pl.when(pl.program_id(0) == 0)
    def _():
        i = lax.broadcasted_iota(jnp.int32, (512, 128), 0)
        side, j = i >> 8, i & 255
        near, far = (j >> 3) & 3, (j >> 1) & 3
        pos = (j >> 5) * 64 + ((resp >> 1) ^ (far * 4 + near)) * 4 + (core ^ side) * 2 + (j & 1)
        bias_ref[...] = jnp.where((pos >= lo) & (pos < hi), 0.0, NEG)
        prow = row0 + (lax.broadcasted_iota(jnp.int32, (512, 128), 1) & 1)
        seen = (pos <= prow) & ((pos >= split) == (prow >= split))
        pbias_ref[...] = jnp.where(seen, 0.0, NEG)

    k_ref[0:256] = km_ref[...].reshape(256, 128)
    k_ref[256:512] = kx_ref[...].reshape(256, 128)
    v_ref[0:256] = vm_ref[...].reshape(256, 128)
    v_ref[256:512] = vx_ref[...].reshape(256, 128)
    K, V = k_ref[...], v_ref[...]
    KT = K.T

    zero = jnp.zeros((112, 128), f32)

    def rows16(ref):
        x = ref[...].astype(f32)
        return jnp.concatenate([x[:, g * 128 : g * 128 + 128] for g in range(8)] + [zero], axis=0)

    pq, pg, po = rows16(pq_ref), rows16(pg_ref), rows16(po_ref)
    delta = row_delta(pg, po)[0:1]
    pq, pg = pq.astype(bf), pg.astype(bf)
    S = dot_t(K, pq) + pbias_ref[...]
    m = jnp.max(S, axis=0, keepdims=True) * C2
    e = jnp.exp2(S * C2 - m)
    p = e * (1.0 / jnp.sum(e, axis=0, keepdims=True))
    ds = (p * (dot_t(V, pg) - delta)).astype(bf)
    dv_ref[0:512] = dot(p.astype(bf), pg)
    dk_ref[0:512] = dot(ds, pq)
    pdq = dot(KT, ds).T * SCALE
    for g in range(8):
        pdq_ref[:, g * 128 : g * 128 + 128] = pdq[2 * g : 2 * g + 2].astype(bf)

    @pl.loop(0, 1024 // CH)
    def _(i):
        rows = pl.ds(pl.multiple_of(i * CH, CH), CH)
        Q, G = qs_ref[0, rows], gs_ref[0, rows]
        m_own, l_own, delta = st_ref[0, 0:1, rows], st_ref[0, 8:9, rows], st_ref[0, 16:17, rows]
        S = dot_t(K, Q) + jnp.concatenate([bias_ref[...]] * (CH // 128), axis=1)
        m = jnp.maximum(jnp.max(S, axis=0, keepdims=True) * C2, m_own)
        e = jnp.exp2(S * C2 - m)
        total = jnp.sum(e, axis=0, keepdims=True) + l_own * jnp.exp2(m_own - m)
        lse_ref[0, :, rows] = jnp.broadcast_to(m + jnp.log2(total), (8, CH))
        p = e * (1.0 / total)
        ds = (p * (dot_t(V, G) - delta)).astype(bf)
        dv_ref[0:512] += dot(p.astype(bf), G)
        dk_ref[0:512] += dot(ds, Q)
        dqt_ref[0, :, rows] = dot(KT, ds)

    for k in range(16):
        place = (resp >> 1) ^ ((k & 3) * 4 + (k >> 2))
        for dst, base in ((dm_ref, 0), (dx_ref, 256)):
            rows = [pl.ds(base + 2 * k + r, 8, stride=32) for r in range(2)]
            key = jnp.concatenate([dk_ref[i, :] for i in rows], axis=0)
            value = jnp.concatenate([dv_ref[i, :] for i in rows], axis=0)
            dst[place, 0] = (key * SCALE).astype(bf)
            dst[place, 1] = value.astype(bf)


def own_grads_kernel(CH, qs_ref, gs_ref, st_ref, lse_ref, dqt_ref, k_ref, v_ref, dq_ref, d_ref, bias_ref, dk_ref, dv_ref):
    @pl.when(pl.program_id(0) == 0)
    def _():
        bias_ref[...] = causal_bias(lax.axis_index("ctx"))

    K, V = k_ref[...].reshape(1024, 128), v_ref[...].reshape(1024, 128)
    KT = K.T
    dk_ref[...] = jnp.zeros((1024, 128), f32)
    dv_ref[...] = jnp.zeros((1024, 128), f32)

    @pl.loop(0, 1024 // CH)
    def _(i):
        rows = pl.ds(pl.multiple_of(i * CH, CH), CH)
        Q, G = qs_ref[0, rows], gs_ref[0, rows]
        S = dot_t(K, Q) + jnp.concatenate([bias_ref[...]] * (CH // 128), axis=1)
        p = jnp.exp2(S * C2 - lse_ref[0, 0:1, rows])
        ds = (p * (dot_t(V, G) - st_ref[0, 16:17, rows])).astype(bf)
        dv_ref[...] += dot(p.astype(bf), G)
        dk_ref[...] += dot(ds, Q)
        dq = ((dqt_ref[0, :, rows] + dot(KT, ds)) * SCALE).T
        for j in range(CH // 128):
            lanes = pl.ds(pl.multiple_of(i * CH + j * 128, 128), 128)
            dq_ref[:, lanes] = dq[j * 128 : j * 128 + 128].astype(bf)

    d_ref[:, 0:128] = (dk_ref[...] * SCALE).astype(bf).reshape(8, 128, 128)
    d_ref[:, 128:256] = dv_ref[...].astype(bf).reshape(8, 128, 128)


SMEM = pl.BlockSpec(memory_space=pltpu.SMEM)


def wide(n):
    return pl.BlockSpec((n, 1024), lambda h: (0, h))


def per_head(*shape):
    return pl.BlockSpec((1,) + shape, lambda h: (h, 0, 0))


def own_block(kv):
    return pl.BlockSpec((8, 128, 128), lambda h: (0, 2 * h + kv, 0))


def pack_block(kv):
    return pl.BlockSpec((8, 1, 32, 128), lambda h: (0, 2 * h + kv, 0, 0))


def shape_of(*shape, dtype=bf):
    return jax.ShapeDtypeStruct(shape, dtype)


def cost(gflops, megabytes):
    return pl.CostEstimate(flops=int(gflops * 1e9), bytes_accessed=int(megabytes * 2**20), transcendentals=0)


def own_stats(length, q, g, o, own, CH=1024):
    return pl.pallas_call(
        functools.partial(own_stats_kernel, CH),
        grid=(4,),
        in_specs=[SMEM, wide(128), wide(128), wide(128), own_block(0)],
        out_specs=[per_head(1024, 128), per_head(1024, 128), per_head(24, 1024)],
        out_shape=[shape_of(4, 1024, 128), shape_of(4, 1024, 128), shape_of(4, 24, 1024, dtype=f32)],
        scratch_shapes=[pltpu.VMEM((1024, 128), f32)],
        compiler_params=LIMIT,
        cost_estimate=cost(1.2, 6),
    )(length, q, g, o, own)


def prefix(prompt, offset, qs, gs, st, mine, other, pq, pg, po, CH=1024):
    big = pl.BlockSpec((16, 2, 16, 128), lambda h: (0, h, 0, 0))
    return pl.pallas_call(
        functools.partial(prefix_kernel, CH),
        grid=(4,),
        in_specs=[SMEM, SMEM, per_head(1024, 128), per_head(1024, 128), per_head(24, 1024),
                  pack_block(0), pack_block(1), pack_block(0), pack_block(1), wide(2), wide(2), wide(2)],
        out_specs=[big, big, per_head(128, 1024), per_head(8, 1024), wide(2)],
        out_shape=[shape_of(16, 8, 16, 128), shape_of(16, 8, 16, 128), shape_of(4, 128, 1024, dtype=f32),
                   shape_of(4, 8, 1024, dtype=f32), shape_of(2, 4096)],
        scratch_shapes=[pltpu.VMEM((512, 128), f32), pltpu.VMEM((512, 128), f32), pltpu.VMEM((512, 128), bf),
                        pltpu.VMEM((512, 128), bf), pltpu.VMEM((544, 128), f32), pltpu.VMEM((544, 128), f32)],
        compiler_params=LIMIT,
        cost_estimate=cost(2.7, 8),
    )(prompt, offset, qs, gs, st, mine, mine, other, other, pq, pg, po)


def own_grads(qs, gs, st, lse, dqt, own, CH=1024):
    return pl.pallas_call(
        functools.partial(own_grads_kernel, CH),
        grid=(4,),
        in_specs=[per_head(1024, 128), per_head(1024, 128), per_head(24, 1024), per_head(8, 1024), per_head(128, 1024),
                  own_block(0), own_block(1)],
        out_specs=[wide(128), pl.BlockSpec((8, 256, 128), lambda h: (0, h, 0))],
        out_shape=[shape_of(128, 4096), shape_of(8, 1040, 128)],
        scratch_shapes=[pltpu.VMEM((1024, 128), f32)] * 3,
        compiler_params=LIMIT,
        cost_estimate=cost(5.4, 10),
    )(qs, gs, st, lse, dqt, own, own)


def copies_kernel(key_ref, value_ref, pack_key_ref, pack_value_ref, out_ref, pack_ref, block, rows, sems):
    taken = [pltpu.make_async_copy(pack_key_ref, rows.at[0], sems.at[16]), pltpu.make_async_copy(pack_value_ref, rows.at[1], sems.at[17])]
    for h in range(4):
        for kv, ref in enumerate((key_ref, value_ref)):
            i = 2 * h + kv
            source = ref.at[:, pl.ds(h * 128, 128)]
            taken.append(pltpu.make_async_copy(source, block.at[pl.ds(i * 128, 128)], sems.at[8 + i]))
    for copy in taken:
        copy.start()
    for copy in taken:
        copy.wait()
    sent = [pltpu.make_async_copy(block, out_ref.at[i], sems.at[i]) for i in range(8)]
    for copy in sent:
        copy.start()
    both = rows[...].astype(f32)
    parts = [both[kv][:, h * 128 : h * 128 + 128] for h in range(4) for kv in range(2)]
    pack_ref[...] = jnp.concatenate(parts, axis=0).astype(bf)
    for copy in sent:
        copy.wait()


def copies_of(key, value, pack_key, pack_value):
    return pl.pallas_call(
        copies_kernel,
        in_specs=[pl.BlockSpec(memory_space=pltpu.HBM)] * 4,
        out_specs=[pl.BlockSpec(memory_space=pl.ANY), pl.BlockSpec(memory_space=pltpu.VMEM)],
        out_shape=[shape_of(8, 1024, 128), shape_of(16, 128)],
        scratch_shapes=[pltpu.VMEM((1024, 128), bf), pltpu.VMEM((2, 2, 512), bf), pltpu.SemaphoreType.DMA((18,))],
        compiler_params=LIMIT,
        cost_estimate=cost(0, 2),
    )(key, value, pack_key, pack_value)


def regroup_kernel(*refs):
    x = jnp.concatenate([ref[...].astype(f32) for ref in refs[:4]], axis=0)
    for k in range(8):
        rows = [x[16 * i + 2 * k : 16 * i + 2 * k + 2] for i in range(16)]
        rows = jnp.concatenate(rows, axis=0).astype(bf)
        for c in range(8):
            refs[4][c, k] = rows


def regroup(*blocks):
    return pl.pallas_call(
        regroup_kernel,
        out_shape=shape_of(8, 8, 32, 128),
        compiler_params=SMALL,
        cost_estimate=cost(0, 1),
    )(*blocks)


PACK_ROWS = pl.BlockSpec((8, 16, 128), lambda *_: (0, 64, 0))


def patch_kernel(big_ref, parts_ref, out_ref, total_ref):
    total_ref[0:128] = jnp.sum(parts_ref[...].astype(f32), axis=0).reshape(128, 128)
    for c in range(8):
        out_ref[c] = total_ref[pl.ds(c, 16, stride=8), :].astype(bf)


def patch(big, parts):
    return pl.pallas_call(
        patch_kernel,
        grid=(1,),
        in_specs=[pl.BlockSpec(memory_space=pl.ANY), pl.BlockSpec((16, 8, 16, 128), lambda i: (0, 0, 0, 0))],
        out_specs=PACK_ROWS,
        out_shape=shape_of(8, 1040, 128),
        scratch_shapes=[pltpu.VMEM((136, 128), f32)],
        input_output_aliases={0: 0},
        compiler_params=LIMIT,
        cost_estimate=cost(0, 1),
    )(big, parts)


def finish_kernel(parts_ref, pack_ref, key_ref, value_ref, pack_key_ref, pack_value_ref):
    total = jnp.sum(parts_ref[...].astype(f32), axis=0)
    key_ref[...] = total[0:128].astype(bf)
    value_ref[...] = total[128:256].astype(bf)

    @pl.when(pl.program_id(0) == 0)
    def _():
        rows = jnp.sum(pack_ref[...].astype(f32), axis=0)
        pack_key_ref[...] = jnp.concatenate([rows[4 * h : 4 * h + 2] for h in range(4)], axis=1).astype(bf)
        pack_value_ref[...] = jnp.concatenate([rows[4 * h + 2 : 4 * h + 4] for h in range(4)], axis=1).astype(bf)


def finish(parts):
    column = pl.BlockSpec((128, 128), lambda h: (0, h))
    whole = pl.BlockSpec((2, 512), lambda h: (0, 0))
    return pl.pallas_call(
        finish_kernel,
        grid=(4,),
        in_specs=[pl.BlockSpec((8, 256, 128), lambda h: (0, h, 0)), PACK_ROWS],
        out_specs=[column, column, whole, whole],
        out_shape=[shape_of(128, 512), shape_of(128, 512), shape_of(2, 512), shape_of(2, 512)],
        compiler_params=SMALL,
        cost_estimate=cost(0, 3),
    )(parts, parts)


YZ = [[c + 2 * i for i in range(16)] for c in range(2)]


def from_partner(block, mask):
    return lax.ppermute(block, "resp", [(i, i ^ mask) for i in range(32)])


def exchange(blocks, axis="ctx", groups=None):
    return lax.all_to_all(blocks, axis, 0, 0, tiled=True, axis_index_groups=groups)


def shards(
    resp_query, resp_key, resp_value, resp_out, resp_grad,
    pack_query, pack_key, pack_value, pack_out, pack_grad,
    resp_length, prompt_id, pack_offset,
):
    copies, block = copies_of(resp_key[0], resp_value[0], pack_key, pack_value)
    own = exchange(copies)
    block = jnp.concatenate([block] + [from_partner(block, m) for m in (8, 16, 24)], axis=0)
    mine = exchange(regroup(block, *[from_partner(block, m) for m in (2, 4, 6)]))
    qs, gs, st = own_stats(resp_length, resp_query[0], resp_grad[0], resp_out[0], own)
    mine, st = lax.optimization_barrier((mine, st))
    other = from_partner(mine, 1)
    dmine, dother, dqt, lse, pdq = prefix(
        prompt_id, pack_offset, qs, gs, st, mine, other, pack_query, pack_grad, pack_out
    )
    both = dmine.astype(f32) + from_partner(dother, 1).astype(f32)
    parts = exchange(both.astype(bf), "resp", YZ)
    dq, down = own_grads(qs, gs, st, lse, dqt, own)
    key, value, block_key, block_value = finish(exchange(patch(down, parts)))
    return dq[None], key[None], value[None], pdq, block_key, block_value


def solution(mesh):
    long = P("resp", "ctx", None)
    pack = P(("ctx", "resp"), None)
    return jax.shard_map(
        shards,
        mesh=mesh,
        in_specs=(long,) * 5 + (pack,) * 5 + (P("resp"), P("resp"), P()),
        out_specs=(long,) * 3 + (pack,) * 3,
        check_vma=False,
    )
```

```python
import functools
import math

import jax
import jax.numpy as jnp
from jax import lax
from jax.experimental import pallas as pl
from jax.experimental.pallas import tpu as pltpu
from jax.sharding import PartitionSpec as P

bf, f32 = jnp.bfloat16, jnp.float32
SCALE = 128 ** -0.5
C2 = SCALE * math.log2(math.e)
NEG = -1e30
LIMIT = pltpu.CompilerParams(vmem_limit_bytes=60 * 1024 * 1024)
SMALL = pltpu.CompilerParams(vmem_limit_bytes=12 * 1024 * 1024)


def dot_t(a, b):
    return lax.dot_general(a, b, (((1,), (1,)), ((), ())), preferred_element_type=f32)


def dot(a, b):
    return jnp.dot(a, b, preferred_element_type=f32)


def row_delta(grad, out):
    prod = grad * out
    high = prod.astype(bf)
    low = (prod - high.astype(f32)).astype(bf)
    return dot_t(jnp.ones((8, 256), bf), jnp.concatenate([high, low], axis=1))


def causal_bias(ctx):
    u = lax.broadcasted_iota(jnp.int32, (1024, 128), 0)
    r = lax.broadcasted_iota(jnp.int32, (1024, 128), 1)
    return jnp.where(u <= ctx * 128 + r, 0.0, NEG)


def own_stats_kernel(CH, len_ref, q_ref, g_ref, o_ref, k_ref, qs_ref, gs_ref, st_ref, bias_ref):
    @pl.when(pl.program_id(0) == 0)
    def _():
        bias_ref[...] = causal_bias(lax.axis_index("ctx"))

    live = len_ref[0] - lax.axis_index("ctx") * 128
    rr = lax.broadcasted_iota(jnp.int32, (128, 128), 0)
    for g in range(8):
        s = slice(g * 128, g * 128 + 128)
        qs_ref[0, s] = q_ref[:, s]
        grad = jnp.where(rr < live, g_ref[:, s].astype(f32), 0.0)
        gs_ref[0, s] = grad.astype(bf)
        st_ref[0, 16:24, s] = row_delta(grad, o_ref[:, s].astype(f32))

    K = k_ref[...].reshape(1024, 128)

    @pl.loop(0, 1024 // CH)
    def _(i):
        rows = pl.ds(pl.multiple_of(i * CH, CH), CH)
        S = dot_t(K, qs_ref[0, rows]) + jnp.concatenate([bias_ref[...]] * (CH // 128), axis=1)
        m = jnp.max(S, axis=0, keepdims=True) * C2
        total = jnp.sum(jnp.exp2(S * C2 - m), axis=0, keepdims=True)
        st_ref[0, 0:8, rows] = jnp.broadcast_to(m, (8, CH))
        st_ref[0, 8:16, rows] = jnp.broadcast_to(total, (8, CH))


def prefix_kernel(CH, prompt_ref, offset_ref, qs_ref, gs_ref, st_ref, km_ref, vm_ref, kx_ref, vx_ref, pq_ref, pg_ref, po_ref,
                  dm_ref, dx_ref, dqt_ref, lse_ref, pdq_ref, bias_ref, pbias_ref, k_ref, v_ref, dk_ref, dv_ref):
    resp = lax.axis_index("resp")
    core, row0 = resp & 1, (lax.axis_index("ctx") * 32 + resp) * 2
    split = offset_ref[1]
    lo = jnp.where(prompt_ref[0] == 0, 0, split)
    hi = jnp.where(prompt_ref[0] == 0, split, 512)

    @pl.when(pl.program_id(0) == 0)
    def _():
        i = lax.broadcasted_iota(jnp.int32, (512, 128), 0)
        side, j = i >> 8, i & 255
        pos = (j >> 5) * 64 + ((resp >> 1) ^ ((j >> 1) & 15)) * 4 + (core ^ side) * 2 + (j & 1)
        bias_ref[...] = jnp.where((pos >= lo) & (pos < hi), 0.0, NEG)
        prow = row0 + (lax.broadcasted_iota(jnp.int32, (512, 128), 1) & 1)
        seen = (pos <= prow) & ((pos >= split) == (prow >= split))
        pbias_ref[...] = jnp.where(seen, 0.0, NEG)

    k_ref[0:256] = km_ref[...].reshape(256, 128)
    k_ref[256:512] = kx_ref[...].reshape(256, 128)
    v_ref[0:256] = vm_ref[...].reshape(256, 128)
    v_ref[256:512] = vx_ref[...].reshape(256, 128)
    K, V = k_ref[...], v_ref[...]
    KT = K.T

    zero = jnp.zeros((112, 128), f32)

    def rows16(ref):
        x = ref[...].astype(f32)
        return jnp.concatenate([x[:, g * 128 : g * 128 + 128] for g in range(8)] + [zero], axis=0)

    pq, pg, po = rows16(pq_ref), rows16(pg_ref), rows16(po_ref)
    delta = row_delta(pg, po)[0:1]
    pq, pg = pq.astype(bf), pg.astype(bf)
    S = dot_t(K, pq) + pbias_ref[...]
    m = jnp.max(S, axis=0, keepdims=True) * C2
    e = jnp.exp2(S * C2 - m)
    p = e * (1.0 / jnp.sum(e, axis=0, keepdims=True))
    ds = (p * (dot_t(V, pg) - delta)).astype(bf)
    dv_ref[...] = dot(p.astype(bf), pg)
    dk_ref[...] = dot(ds, pq)
    pdq = dot(KT, ds).T * SCALE
    for g in range(8):
        pdq_ref[:, g * 128 : g * 128 + 128] = pdq[2 * g : 2 * g + 2].astype(bf)

    @pl.loop(0, 1024 // CH)
    def _(i):
        rows = pl.ds(pl.multiple_of(i * CH, CH), CH)
        Q, G = qs_ref[0, rows], gs_ref[0, rows]
        m_own, l_own, delta = st_ref[0, 0:1, rows], st_ref[0, 8:9, rows], st_ref[0, 16:17, rows]
        S = dot_t(K, Q) + jnp.concatenate([bias_ref[...]] * (CH // 128), axis=1)
        m = jnp.maximum(jnp.max(S, axis=0, keepdims=True) * C2, m_own)
        e = jnp.exp2(S * C2 - m)
        total = jnp.sum(e, axis=0, keepdims=True) + l_own * jnp.exp2(m_own - m)
        lse_ref[0, :, rows] = jnp.broadcast_to(m + jnp.log2(total), (8, CH))
        p = e * (1.0 / total)
        ds = (p * (dot_t(V, G) - delta)).astype(bf)
        dv_ref[...] += dot(p.astype(bf), G)
        dk_ref[...] += dot(ds, Q)
        dqt_ref[0, :, rows] = dot(KT, ds)

    for dst, s in ((dm_ref, slice(0, 256)), (dx_ref, slice(256, 512))):
        dst[:, 0] = (dk_ref[s] * SCALE).astype(bf).reshape(8, 32, 128)
        dst[:, 1] = dv_ref[s].astype(bf).reshape(8, 32, 128)


def own_grads_kernel(CH, qs_ref, gs_ref, st_ref, lse_ref, dqt_ref, k_ref, v_ref, dq_ref, d_ref, bias_ref, dk_ref, dv_ref):
    @pl.when(pl.program_id(0) == 0)
    def _():
        bias_ref[...] = causal_bias(lax.axis_index("ctx"))

    K, V = k_ref[...].reshape(1024, 128), v_ref[...].reshape(1024, 128)
    KT = K.T
    dk_ref[...] = jnp.zeros((1024, 128), f32)
    dv_ref[...] = jnp.zeros((1024, 128), f32)

    @pl.loop(0, 1024 // CH)
    def _(i):
        rows = pl.ds(pl.multiple_of(i * CH, CH), CH)
        Q, G = qs_ref[0, rows], gs_ref[0, rows]
        S = dot_t(K, Q) + jnp.concatenate([bias_ref[...]] * (CH // 128), axis=1)
        p = jnp.exp2(S * C2 - lse_ref[0, 0:1, rows])
        ds = (p * (dot_t(V, G) - st_ref[0, 16:17, rows])).astype(bf)
        dv_ref[...] += dot(p.astype(bf), G)
        dk_ref[...] += dot(ds, Q)
        dq = ((dqt_ref[0, :, rows] + dot(KT, ds)) * SCALE).T
        for j in range(CH // 128):
            lanes = pl.ds(pl.multiple_of(i * CH + j * 128, 128), 128)
            dq_ref[:, lanes] = dq[j * 128 : j * 128 + 128].astype(bf)

    d_ref[:, 0:128] = (dk_ref[...] * SCALE).astype(bf).reshape(8, 128, 128)
    d_ref[:, 128:256] = dv_ref[...].astype(bf).reshape(8, 128, 128)


SMEM = pl.BlockSpec(memory_space=pltpu.SMEM)


def wide(n):
    return pl.BlockSpec((n, 1024), lambda h: (0, h))


def per_head(*shape):
    return pl.BlockSpec((1,) + shape, lambda h: (h, 0, 0))


def own_block(kv):
    return pl.BlockSpec((8, 128, 128), lambda h: (0, 2 * h + kv, 0))


def pack_block(kv):
    return pl.BlockSpec((8, 1, 32, 128), lambda h: (0, 2 * h + kv, 0, 0))


def shape_of(*shape, dtype=bf):
    return jax.ShapeDtypeStruct(shape, dtype)


def cost(gflops, megabytes):
    return pl.CostEstimate(flops=int(gflops * 1e9), bytes_accessed=int(megabytes * 2**20), transcendentals=0)


def own_stats(length, q, g, o, own, CH=1024):
    return pl.pallas_call(
        functools.partial(own_stats_kernel, CH),
        grid=(4,),
        in_specs=[SMEM, wide(128), wide(128), wide(128), own_block(0)],
        out_specs=[per_head(1024, 128), per_head(1024, 128), per_head(24, 1024)],
        out_shape=[shape_of(4, 1024, 128), shape_of(4, 1024, 128), shape_of(4, 24, 1024, dtype=f32)],
        scratch_shapes=[pltpu.VMEM((1024, 128), f32)],
        compiler_params=LIMIT,
        cost_estimate=cost(1.2, 6),
    )(length, q, g, o, own)


def prefix(prompt, offset, qs, gs, st, mine, other, pq, pg, po, CH=1024):
    big = pl.BlockSpec((8, 2, 32, 128), lambda h: (0, h, 0, 0))
    return pl.pallas_call(
        functools.partial(prefix_kernel, CH),
        grid=(4,),
        in_specs=[SMEM, SMEM, per_head(1024, 128), per_head(1024, 128), per_head(24, 1024),
                  pack_block(0), pack_block(1), pack_block(0), pack_block(1), wide(2), wide(2), wide(2)],
        out_specs=[big, big, per_head(128, 1024), per_head(8, 1024), wide(2)],
        out_shape=[shape_of(8, 8, 32, 128), shape_of(8, 8, 32, 128), shape_of(4, 128, 1024, dtype=f32),
                   shape_of(4, 8, 1024, dtype=f32), shape_of(2, 4096)],
        scratch_shapes=[pltpu.VMEM((512, 128), f32), pltpu.VMEM((512, 128), f32), pltpu.VMEM((512, 128), bf),
                        pltpu.VMEM((512, 128), bf), pltpu.VMEM((512, 128), f32), pltpu.VMEM((512, 128), f32)],
        compiler_params=LIMIT,
        cost_estimate=cost(2.7, 8),
    )(prompt, offset, qs, gs, st, mine, mine, other, other, pq, pg, po)


def own_grads(qs, gs, st, lse, dqt, own, CH=1024):
    return pl.pallas_call(
        functools.partial(own_grads_kernel, CH),
        grid=(4,),
        in_specs=[per_head(1024, 128), per_head(1024, 128), per_head(24, 1024), per_head(8, 1024), per_head(128, 1024),
                  own_block(0), own_block(1)],
        out_specs=[wide(128), pl.BlockSpec((8, 256, 128), lambda h: (0, h, 0))],
        out_shape=[shape_of(128, 4096), shape_of(8, 1024, 128)],
        scratch_shapes=[pltpu.VMEM((1024, 128), f32)] * 3,
        compiler_params=LIMIT,
        cost_estimate=cost(5.4, 10),
    )(qs, gs, st, lse, dqt, own, own)


def copies_kernel(key_ref, value_ref, pack_key_ref, pack_value_ref, out_ref, pack_ref, block, rows, sems):
    taken = [pltpu.make_async_copy(pack_key_ref, rows.at[0], sems.at[16]), pltpu.make_async_copy(pack_value_ref, rows.at[1], sems.at[17])]
    for h in range(4):
        for kv, ref in enumerate((key_ref, value_ref)):
            i = 2 * h + kv
            source = ref.at[:, pl.ds(h * 128, 128)]
            taken.append(pltpu.make_async_copy(source, block.at[pl.ds(i * 128, 128)], sems.at[8 + i]))
    for copy in taken:
        copy.start()
    for copy in taken:
        copy.wait()
    sent = [pltpu.make_async_copy(block, out_ref.at[i], sems.at[i]) for i in range(8)]
    for copy in sent:
        copy.start()
    both = rows[...].astype(f32)
    parts = [both[kv][:, h * 128 : h * 128 + 128] for h in range(4) for kv in range(2)]
    pack_ref[...] = jnp.concatenate(parts, axis=0).astype(bf)
    for copy in sent:
        copy.wait()


def copies_of(key, value, pack_key, pack_value):
    return pl.pallas_call(
        copies_kernel,
        in_specs=[pl.BlockSpec(memory_space=pltpu.HBM)] * 4,
        out_specs=[pl.BlockSpec(memory_space=pl.ANY), pl.BlockSpec(memory_space=pltpu.VMEM)],
        out_shape=[shape_of(8, 1024, 128), shape_of(16, 128)],
        scratch_shapes=[pltpu.VMEM((1024, 128), bf), pltpu.VMEM((2, 2, 512), bf), pltpu.SemaphoreType.DMA((18,))],
        compiler_params=LIMIT,
        cost_estimate=cost(0, 2),
    )(key, value, pack_key, pack_value)


def regroup_kernel(*refs):
    x = jnp.concatenate([ref[...].astype(f32) for ref in refs[:4]], axis=0)
    for k in range(8):
        rows = [x[16 * i + 2 * k : 16 * i + 2 * k + 2] for i in range(16)]
        rows = jnp.concatenate(rows, axis=0).astype(bf)
        for c in range(8):
            refs[4][c, k] = rows


def regroup(*blocks):
    return pl.pallas_call(
        regroup_kernel,
        out_shape=shape_of(8, 8, 32, 128),
        compiler_params=SMALL,
        cost_estimate=cost(0, 1),
    )(*blocks)


def ungroup_kernel(parts_ref, *refs):
    total = jnp.sum(parts_ref[...].astype(f32), axis=0)
    for m in range(4):
        rows = [total[k, 8 * i + 2 * m : 8 * i + 2 * m + 2] for i in range(4) for k in range(8)]
        refs[m][...] = jnp.concatenate(rows, axis=0).astype(bf)


def ungroup(parts):
    return pl.pallas_call(
        ungroup_kernel,
        out_shape=[shape_of(64, 128)] * 4,
        compiler_params=SMALL,
        cost_estimate=cost(0, 1),
    )(parts)


def quarter_kernel(*refs):
    total = sum(ref[...].astype(f32) for ref in refs[:4])
    for m in range(4):
        refs[4 + m][...] = total[16 * m : 16 * m + 16].astype(bf)


def quarter(*blocks):
    return pl.pallas_call(
        quarter_kernel,
        out_shape=[shape_of(16, 128)] * 4,
        compiler_params=SMALL,
        cost_estimate=cost(0, 0.1),
    )(*blocks)


def finish_pack_kernel(a_ref, b_ref, c_ref, d_ref, key_ref, value_ref):
    rows = sum(ref[...].astype(f32) for ref in (a_ref, b_ref, c_ref, d_ref))
    key_ref[...] = jnp.concatenate([rows[4 * h : 4 * h + 2] for h in range(4)], axis=1).astype(bf)
    value_ref[...] = jnp.concatenate([rows[4 * h + 2 : 4 * h + 4] for h in range(4)], axis=1).astype(bf)


def finish_pack(*blocks):
    return pl.pallas_call(finish_pack_kernel, out_shape=[shape_of(2, 512)] * 2, compiler_params=SMALL, cost_estimate=cost(0, 0.1))(*blocks)


def finish_own_kernel(parts_ref, key_ref, value_ref):
    total = jnp.sum(parts_ref[...].astype(f32), axis=0)
    key_ref[...] = total[0:128].astype(bf)
    value_ref[...] = total[128:256].astype(bf)


def finish_own(parts):
    column = pl.BlockSpec((128, 128), lambda h: (0, h))
    return pl.pallas_call(
        finish_own_kernel,
        grid=(4,),
        in_specs=[pl.BlockSpec((8, 256, 128), lambda h: (0, h, 0))],
        out_specs=[column, column],
        out_shape=[shape_of(128, 512), shape_of(128, 512)],
        compiler_params=SMALL,
        cost_estimate=cost(0, 3),
    )(parts)


def from_partner(block, mask):
    return lax.ppermute(block, "resp", [(i, i ^ mask) for i in range(32)])


def exchange(blocks):
    return lax.all_to_all(blocks, "ctx", 0, 0, tiled=True)


def shards(
    resp_query, resp_key, resp_value, resp_out, resp_grad,
    pack_query, pack_key, pack_value, pack_out, pack_grad,
    resp_length, prompt_id, pack_offset,
):
    copies, block = copies_of(resp_key[0], resp_value[0], pack_key, pack_value)
    own = exchange(copies)
    block = jnp.concatenate([block] + [from_partner(block, m) for m in (2, 4, 6)], axis=0)
    mine = exchange(regroup(block, *[from_partner(block, m) for m in (8, 16, 24)]))
    qs, gs, st = own_stats(resp_length, resp_query[0], resp_grad[0], resp_out[0], own)
    mine, st = lax.optimization_barrier((mine, st))
    other = from_partner(mine, 1)
    dmine, dother, dqt, lse, pdq = prefix(
        prompt_id, pack_offset, qs, gs, st, mine, other, pack_query, pack_grad, pack_out
    )
    both = dmine.astype(f32) + from_partner(dother, 1).astype(f32)
    parts = exchange(both.astype(bf))
    dq, down = own_grads(qs, gs, st, lse, dqt, own)
    parts = ungroup(parts)
    own_parts = exchange(down)
    parts = quarter(parts[0], *[from_partner(parts[m], 2 * m) for m in (1, 2, 3)])
    block_key, block_value = finish_pack(parts[0], *[from_partner(parts[m], 8 * m) for m in (1, 2, 3)])
    key, value = finish_own(own_parts)
    return dq[None], key[None], value[None], pdq, block_key, block_value


def solution(mesh):
    long = P("resp", "ctx", None)
    pack = P(("ctx", "resp"), None)
    return jax.shard_map(
        shards,
        mesh=mesh,
        in_specs=(long,) * 5 + (pack,) * 5 + (P("resp"), P("resp"), P()),
        out_specs=(long,) * 3 + (pack,) * 3,
        check_vma=False,
    )
```

```python
import functools
import math

import jax
import jax.numpy as jnp
from jax import lax
from jax.experimental import pallas as pl
from jax.experimental.pallas import tpu as pltpu
from jax.sharding import PartitionSpec as P

bf, f32 = jnp.bfloat16, jnp.float32
SCALE = 128 ** -0.5
C2 = SCALE * math.log2(math.e)
NEG = -1e30
LIMIT = pltpu.CompilerParams(vmem_limit_bytes=60 * 1024 * 1024)
SMALL = pltpu.CompilerParams(vmem_limit_bytes=12 * 1024 * 1024)


def dot_t(a, b):
    return lax.dot_general(a, b, (((1,), (1,)), ((), ())), preferred_element_type=f32)


def dot(a, b):
    return jnp.dot(a, b, preferred_element_type=f32)


def row_delta(grad, out):
    prod = grad * out
    high = prod.astype(bf)
    low = (prod - high.astype(f32)).astype(bf)
    return dot_t(jnp.ones((8, 256), bf), jnp.concatenate([high, low], axis=1))


def causal_bias(ctx):
    u = lax.broadcasted_iota(jnp.int32, (1024, 128), 0)
    r = lax.broadcasted_iota(jnp.int32, (1024, 128), 1)
    return jnp.where(u <= ctx * 128 + r, 0.0, NEG)


def own_stats_kernel(CH, len_ref, q_ref, g_ref, o_ref, k_ref, qs_ref, gs_ref, st_ref, bias_ref):
    @pl.when(pl.program_id(0) == 0)
    def _():
        bias_ref[...] = causal_bias(lax.axis_index("ctx"))

    live = len_ref[0] - lax.axis_index("ctx") * 128
    rr = lax.broadcasted_iota(jnp.int32, (128, 128), 0)
    for g in range(8):
        s = slice(g * 128, g * 128 + 128)
        qs_ref[0, s] = q_ref[:, s]
        grad = jnp.where(rr < live, g_ref[:, s].astype(f32), 0.0)
        gs_ref[0, s] = grad.astype(bf)
        st_ref[0, 16:24, s] = row_delta(grad, o_ref[:, s].astype(f32))

    K = k_ref[...].reshape(1024, 128)

    @pl.loop(0, 1024 // CH)
    def _(i):
        rows = pl.ds(pl.multiple_of(i * CH, CH), CH)
        S = dot_t(K, qs_ref[0, rows]) + jnp.concatenate([bias_ref[...]] * (CH // 128), axis=1)
        m = jnp.max(S, axis=0, keepdims=True) * C2
        total = jnp.sum(jnp.exp2(S * C2 - m), axis=0, keepdims=True)
        st_ref[0, 0:8, rows] = jnp.broadcast_to(m, (8, CH))
        st_ref[0, 8:16, rows] = jnp.broadcast_to(total, (8, CH))


def prefix_kernel(HP, prompt_ref, offset_ref, qs_ref, gs_ref, st_ref, km_ref, kx_ref, pq_ref, pg_ref, po_ref,
                  dm_ref, dx_ref, dqt_ref, lse_ref, pdq_ref, bias_ref, pbias_ref):
    resp = lax.axis_index("resp")
    core, row0 = resp & 1, (lax.axis_index("ctx") * 32 + resp) * 2
    split = offset_ref[1]
    lo = jnp.where(prompt_ref[0] == 0, 0, split)
    hi = jnp.where(prompt_ref[0] == 0, split, 512)

    @pl.when(pl.program_id(0) == 0)
    def _():
        i = lax.broadcasted_iota(jnp.int32, (512, 128), 0)
        side, j = i >> 8, i & 255
        pos = (j >> 5) * 64 + ((resp >> 1) ^ ((j >> 1) & 15)) * 4 + (core ^ side) * 2 + (j & 1)
        bias_ref[...] = jnp.where((pos >= lo) & (pos < hi), 0.0, NEG)
        prow = row0 + (lax.broadcasted_iota(jnp.int32, (512, 128), 1) & 1)
        seen = (pos <= prow) & ((pos >= split) == (prow >= split))
        pbias_ref[...] = jnp.where(seen, 0.0, NEG)

    for n in range(HP):
        K, V = [jnp.concatenate([ref[:, 2 * n + kv].reshape(256, 128) for ref in (km_ref, kx_ref)], axis=0) for kv in range(2)]
        KT = K.T

        zero = jnp.zeros((112, 128), f32)

        def rows16(ref):
            x = ref[...].astype(f32)
            return jnp.concatenate([x[:, n * 1024 + g * 128 : n * 1024 + g * 128 + 128] for g in range(8)] + [zero], axis=0)

        pq, pg, po = rows16(pq_ref), rows16(pg_ref), rows16(po_ref)
        delta = row_delta(pg, po)[0:1]
        pq, pg = pq.astype(bf), pg.astype(bf)
        Q = jnp.concatenate([qs_ref[n], pq], axis=0)
        G = jnp.concatenate([gs_ref[n], pg], axis=0)
        low = jnp.full((1, 128), NEG, f32)
        m_own = jnp.concatenate([st_ref[n, 0:1], low], axis=1)
        l_own = jnp.concatenate([st_ref[n, 8:9], jnp.zeros((1, 128), f32)], axis=1)
        both_delta = jnp.concatenate([st_ref[n, 16:17], delta], axis=1)
        S = dot_t(K, Q) + jnp.concatenate([bias_ref[...]] * 8 + [pbias_ref[...]], axis=1)
        m = jnp.maximum(jnp.max(S, axis=0, keepdims=True) * C2, m_own)
        e = jnp.exp2(S * C2 - m)
        total = jnp.sum(e, axis=0, keepdims=True) + l_own * jnp.exp2(m_own - m)
        lse_ref[n] = jnp.broadcast_to((m + jnp.log2(total))[:, 0:1024], (8, 1024))
        p = e * (1.0 / total)
        ds = (p * (dot_t(V, G) - both_delta)).astype(bf)
        dv = dot(p.astype(bf), G)
        dk = dot(ds, Q)
        dq = dot(KT, ds)
        dqt_ref[n] = dq[:, 0:1024]
        pdq = dq[:, 1024:1152].T * SCALE
        for g in range(8):
            pdq_ref[:, n * 1024 + g * 128 : n * 1024 + g * 128 + 128] = pdq[2 * g : 2 * g + 2].astype(bf)

        for dst, s in ((dm_ref, slice(0, 256)), (dx_ref, slice(256, 512))):
            dst[:, 2 * n] = (dk[s] * SCALE).astype(bf).reshape(8, 32, 128)
            dst[:, 2 * n + 1] = dv[s].astype(bf).reshape(8, 32, 128)


def own_grads_kernel(CH, qs_ref, gs_ref, st_ref, lse_ref, dqt_ref, k_ref, v_ref, dq_ref, d_ref, bias_ref, dk_ref, dv_ref):
    @pl.when(pl.program_id(0) == 0)
    def _():
        bias_ref[...] = causal_bias(lax.axis_index("ctx"))

    K, V = k_ref[...].reshape(1024, 128), v_ref[...].reshape(1024, 128)
    KT = K.T
    dk_ref[...] = jnp.zeros((1024, 128), f32)
    dv_ref[...] = jnp.zeros((1024, 128), f32)

    @pl.loop(0, 1024 // CH)
    def _(i):
        rows = pl.ds(pl.multiple_of(i * CH, CH), CH)
        Q, G = qs_ref[0, rows], gs_ref[0, rows]
        S = dot_t(K, Q) + jnp.concatenate([bias_ref[...]] * (CH // 128), axis=1)
        p = jnp.exp2(S * C2 - lse_ref[0, 0:1, rows])
        ds = (p * (dot_t(V, G) - st_ref[0, 16:17, rows])).astype(bf)
        dv_ref[...] += dot(p.astype(bf), G)
        dk_ref[...] += dot(ds, Q)
        dq = ((dqt_ref[0, :, rows] + dot(KT, ds)) * SCALE).T
        for j in range(CH // 128):
            lanes = pl.ds(pl.multiple_of(i * CH + j * 128, 128), 128)
            dq_ref[:, lanes] = dq[j * 128 : j * 128 + 128].astype(bf)

    d_ref[:, 0:128] = (dk_ref[...] * SCALE).astype(bf).reshape(8, 128, 128)
    d_ref[:, 128:256] = dv_ref[...].astype(bf).reshape(8, 128, 128)


SMEM = pl.BlockSpec(memory_space=pltpu.SMEM)


def wide(n):
    return pl.BlockSpec((n, 1024), lambda h: (0, h))


def per_head(*shape):
    return pl.BlockSpec((1,) + shape, lambda h: (h, 0, 0))


def own_block(kv):
    return pl.BlockSpec((8, 128, 128), lambda h: (0, 2 * h + kv, 0))


def shape_of(*shape, dtype=bf):
    return jax.ShapeDtypeStruct(shape, dtype)


def cost(gflops, megabytes):
    return pl.CostEstimate(flops=int(gflops * 1e9), bytes_accessed=int(megabytes * 2**20), transcendentals=0)


def own_stats(length, q, g, o, own, CH=1024):
    return pl.pallas_call(
        functools.partial(own_stats_kernel, CH),
        grid=(4,),
        in_specs=[SMEM, wide(128), wide(128), wide(128), own_block(0)],
        out_specs=[per_head(1024, 128), per_head(1024, 128), per_head(24, 1024)],
        out_shape=[shape_of(4, 1024, 128), shape_of(4, 1024, 128), shape_of(4, 24, 1024, dtype=f32)],
        scratch_shapes=[pltpu.VMEM((1024, 128), f32)],
        compiler_params=LIMIT,
        cost_estimate=cost(1.2, 6),
    )(length, q, g, o, own)


def prefix(prompt, offset, qs, gs, st, mine, other, pq, pg, po, HP=1):
    def heads(*shape):
        return pl.BlockSpec((HP,) + shape, lambda h: (h, 0, 0))

    big = pl.BlockSpec((8, 2 * HP, 32, 128), lambda h: (0, h, 0, 0))
    row = pl.BlockSpec((2, 1024 * HP), lambda h: (0, h))
    return pl.pallas_call(
        functools.partial(prefix_kernel, HP),
        grid=(4 // HP,),
        in_specs=[SMEM, SMEM, heads(1024, 128), heads(1024, 128), heads(24, 1024), big, big, row, row, row],
        out_specs=[big, big, heads(128, 1024), heads(8, 1024), row],
        out_shape=[shape_of(8, 8, 32, 128), shape_of(8, 8, 32, 128), shape_of(4, 128, 1024, dtype=f32),
                   shape_of(4, 8, 1024, dtype=f32), shape_of(2, 4096)],
        scratch_shapes=[pltpu.VMEM((512, 128), f32), pltpu.VMEM((512, 128), f32)],
        compiler_params=LIMIT,
        cost_estimate=cost(2.7, 8),
    )(prompt, offset, qs, gs, st, mine, other, pq, pg, po)


def own_grads(qs, gs, st, lse, dqt, own, CH=1024):
    return pl.pallas_call(
        functools.partial(own_grads_kernel, CH),
        grid=(4,),
        in_specs=[per_head(1024, 128), per_head(1024, 128), per_head(24, 1024), per_head(8, 1024), per_head(128, 1024),
                  own_block(0), own_block(1)],
        out_specs=[wide(128), pl.BlockSpec((8, 256, 128), lambda h: (0, h, 0))],
        out_shape=[shape_of(128, 4096), shape_of(8, 1024, 128)],
        scratch_shapes=[pltpu.VMEM((1024, 128), f32)] * 3,
        compiler_params=LIMIT,
        cost_estimate=cost(5.4, 10),
    )(qs, gs, st, lse, dqt, own, own)


def copies_kernel(key_ref, value_ref, pack_key_ref, pack_value_ref, out_ref, pack_ref, block, rows, sems):
    taken = [pltpu.make_async_copy(pack_key_ref, rows.at[0], sems.at[16]), pltpu.make_async_copy(pack_value_ref, rows.at[1], sems.at[17])]
    for h in range(4):
        for kv, ref in enumerate((key_ref, value_ref)):
            i = 2 * h + kv
            source = ref.at[:, pl.ds(h * 128, 128)]
            taken.append(pltpu.make_async_copy(source, block.at[pl.ds(i * 128, 128)], sems.at[8 + i]))
    for copy in taken:
        copy.start()
    for copy in taken:
        copy.wait()
    sent = [pltpu.make_async_copy(block, out_ref.at[i], sems.at[i]) for i in range(8)]
    for copy in sent:
        copy.start()
    both = rows[...].astype(f32)
    parts = [both[kv][:, h * 128 : h * 128 + 128] for h in range(4) for kv in range(2)]
    pack_ref[...] = jnp.concatenate(parts, axis=0).astype(bf)
    for copy in sent:
        copy.wait()


def copies_of(key, value, pack_key, pack_value):
    return pl.pallas_call(
        copies_kernel,
        in_specs=[pl.BlockSpec(memory_space=pltpu.HBM)] * 4,
        out_specs=[pl.BlockSpec(memory_space=pl.ANY), pl.BlockSpec(memory_space=pltpu.VMEM)],
        out_shape=[shape_of(8, 1024, 128), shape_of(16, 128)],
        scratch_shapes=[pltpu.VMEM((1024, 128), bf), pltpu.VMEM((2, 2, 512), bf), pltpu.SemaphoreType.DMA((18,))],
        compiler_params=LIMIT,
        cost_estimate=cost(0, 2),
    )(key, value, pack_key, pack_value)


def regroup_kernel(*refs):
    x = jnp.concatenate([ref[...].astype(f32) for ref in refs[:-1]], axis=0)
    for k in range(8):
        rows = [x[16 * i + 2 * k : 16 * i + 2 * k + 2] for i in range(16)]
        rows = jnp.concatenate(rows, axis=0).astype(bf)
        for c in range(8):
            refs[-1][c, k] = rows


def regroup(*blocks):
    return pl.pallas_call(
        regroup_kernel,
        out_shape=shape_of(8, 8, 32, 128),
        compiler_params=SMALL,
        cost_estimate=cost(0, 1),
    )(*blocks)


def ungroup_kernel(parts_ref, *refs):
    total = jnp.sum(parts_ref[...].astype(f32), axis=0)
    for m in range(4):
        rows = [total[k, 8 * i + 2 * m : 8 * i + 2 * m + 2] for i in range(4) for k in range(8)]
        refs[m][...] = jnp.concatenate(rows, axis=0).astype(bf)


def ungroup(parts):
    return pl.pallas_call(
        ungroup_kernel,
        out_shape=[shape_of(64, 128)] * 4,
        compiler_params=SMALL,
        cost_estimate=cost(0, 1),
    )(parts)


def quarter_kernel(*refs):
    total = sum(ref[...].astype(f32) for ref in refs[:4])
    for m in range(4):
        refs[4 + m][...] = total[16 * m : 16 * m + 16].astype(bf)


def quarter(*blocks):
    return pl.pallas_call(
        quarter_kernel,
        out_shape=[shape_of(16, 128)] * 4,
        compiler_params=SMALL,
        cost_estimate=cost(0, 0.1),
    )(*blocks)


def finish_pack_kernel(a_ref, b_ref, c_ref, d_ref, key_ref, value_ref):
    rows = sum(ref[...].astype(f32) for ref in (a_ref, b_ref, c_ref, d_ref))
    key_ref[...] = jnp.concatenate([rows[4 * h : 4 * h + 2] for h in range(4)], axis=1).astype(bf)
    value_ref[...] = jnp.concatenate([rows[4 * h + 2 : 4 * h + 4] for h in range(4)], axis=1).astype(bf)


def finish_pack(*blocks):
    return pl.pallas_call(finish_pack_kernel, out_shape=[shape_of(2, 512)] * 2, compiler_params=SMALL, cost_estimate=cost(0, 0.1))(*blocks)


def finish_own_kernel(parts_ref, key_ref, value_ref):
    total = jnp.sum(parts_ref[...].astype(f32), axis=0)
    key_ref[...] = total[0:128].astype(bf)
    value_ref[...] = total[128:256].astype(bf)


def finish_own(parts):
    column = pl.BlockSpec((128, 128), lambda h: (0, h))
    return pl.pallas_call(
        finish_own_kernel,
        grid=(4,),
        in_specs=[pl.BlockSpec((8, 256, 128), lambda h: (0, h, 0))],
        out_specs=[column, column],
        out_shape=[shape_of(128, 512), shape_of(128, 512)],
        compiler_params=SMALL,
        cost_estimate=cost(0, 3),
    )(parts)


def from_partner(block, mask):
    return lax.ppermute(block, "resp", [(i, i ^ mask) for i in range(32)])


def exchange(blocks):
    return lax.all_to_all(blocks, "ctx", 0, 0, tiled=True)


def shards(
    resp_query, resp_key, resp_value, resp_out, resp_grad,
    pack_query, pack_key, pack_value, pack_out, pack_grad,
    resp_length, prompt_id, pack_offset,
):
    copies, block = copies_of(resp_key[0], resp_value[0], pack_key, pack_value)
    own = exchange(copies)
    for mask in (2, 4, 8):
        block = jnp.concatenate([block, from_partner(block, mask)], axis=0)
    mine = exchange(regroup(block, from_partner(block, 16)))
    qs, gs, st = own_stats(resp_length, resp_query[0], resp_grad[0], resp_out[0], own)
    mine, st = lax.optimization_barrier((mine, st))
    other = from_partner(mine, 1)
    dmine, dother, dqt, lse, pdq = prefix(
        prompt_id, pack_offset, qs, gs, st, mine, other, pack_query, pack_grad, pack_out
    )
    both = dmine.astype(f32) + from_partner(dother, 1).astype(f32)
    parts = exchange(both.astype(bf))
    dq, down = own_grads(qs, gs, st, lse, dqt, own)
    parts = ungroup(parts)
    own_parts = exchange(down)
    parts = quarter(parts[0], *[from_partner(parts[m], 2 * m) for m in (1, 2, 3)])
    block_key, block_value = finish_pack(parts[0], *[from_partner(parts[m], 8 * m) for m in (1, 2, 3)])
    key, value = finish_own(own_parts)
    return dq[None], key[None], value[None], pdq, block_key, block_value


def solution(mesh):
    long = P("resp", "ctx", None)
    pack = P(("ctx", "resp"), None)
    return jax.shard_map(
        shards,
        mesh=mesh,
        in_specs=(long,) * 5 + (pack,) * 5 + (P("resp"), P("resp"), P()),
        out_specs=(long,) * 3 + (pack,) * 3,
        check_vma=False,
    )
```

```python
import functools
import math

import jax
import jax.numpy as jnp
from jax import lax
from jax.experimental import pallas as pl
from jax.experimental.pallas import tpu as pltpu
from jax.sharding import PartitionSpec as P

bf, f32 = jnp.bfloat16, jnp.float32
SCALE = 128 ** -0.5
C2 = SCALE * math.log2(math.e)
NEG = -1e30
LIMIT = pltpu.CompilerParams(vmem_limit_bytes=60 * 1024 * 1024)
SMALL = pltpu.CompilerParams(vmem_limit_bytes=12 * 1024 * 1024)


def dot_t(a, b):
    return lax.dot_general(a, b, (((1,), (1,)), ((), ())), preferred_element_type=f32)


def dot(a, b):
    return jnp.dot(a, b, preferred_element_type=f32)


def row_delta(grad, out):
    prod = grad * out
    high = prod.astype(bf)
    low = (prod - high.astype(f32)).astype(bf)
    return dot_t(jnp.ones((8, 256), bf), jnp.concatenate([high, low], axis=1))


def causal_bias(ctx):
    u = lax.broadcasted_iota(jnp.int32, (1024, 128), 0)
    r = lax.broadcasted_iota(jnp.int32, (1024, 128), 1)
    return jnp.where(u <= ctx * 128 + r, 0.0, NEG)


def prepare_kernel(len_ref, q_ref, g_ref, o_ref, qs_ref, gs_ref, delta_ref):
    live = len_ref[0] - lax.axis_index("ctx") * 128
    rr = lax.broadcasted_iota(jnp.int32, (128, 128), 0)
    for g in range(8):
        s = slice(g * 128, g * 128 + 128)
        qs_ref[0, s] = q_ref[:, s]
        grad = jnp.where(rr < live, g_ref[:, s].astype(f32), 0.0)
        gs_ref[0, s] = grad.astype(bf)
        delta_ref[0, :, s] = row_delta(grad, o_ref[:, s].astype(f32))


def own_stats_kernel(qs_ref, k_ref, st_ref, bias_ref):
    @pl.when(pl.program_id(0) == 0)
    def _():
        bias_ref[...] = causal_bias(lax.axis_index("ctx"))

    K = k_ref[...].reshape(1024, 128)
    S = dot_t(K, qs_ref[0]) + jnp.concatenate([bias_ref[...]] * 8, axis=1)
    m = jnp.max(S, axis=0, keepdims=True) * C2
    total = jnp.sum(jnp.exp2(S * C2 - m), axis=0, keepdims=True)
    st_ref[0, 0:8] = jnp.broadcast_to(m, (8, 1024))
    st_ref[0, 8:16] = jnp.broadcast_to(total, (8, 1024))


def prefix_kernel(HP, prompt_ref, offset_ref, qs_ref, gs_ref, st_ref, dl_ref, km_ref, kx_ref, pq_ref, pg_ref, po_ref,
                  d_ref, dqt_ref, lse_ref, pdq_ref, bias_ref, pbias_ref):
    resp = lax.axis_index("resp")
    core, row0 = resp & 1, (lax.axis_index("ctx") * 32 + resp) * 2
    split = offset_ref[1]
    lo = jnp.where(prompt_ref[0] == 0, 0, split)
    hi = jnp.where(prompt_ref[0] == 0, split, 512)

    @pl.when(pl.program_id(0) == 0)
    def _():
        i = lax.broadcasted_iota(jnp.int32, (512, 128), 0)
        side, j = i >> 8, i & 255
        pos = (j >> 5) * 64 + ((resp >> 1) ^ ((j >> 1) & 15)) * 4 + (core ^ side) * 2 + (j & 1)
        bias_ref[...] = jnp.where((pos >= lo) & (pos < hi), 0.0, NEG)
        prow = row0 + (lax.broadcasted_iota(jnp.int32, (512, 128), 1) & 1)
        seen = (pos <= prow) & ((pos >= split) == (prow >= split))
        pbias_ref[...] = jnp.where(seen, 0.0, NEG)

    for n in range(HP):
        K, V = [jnp.concatenate([ref[:, 2 * n + kv].reshape(256, 128) for ref in (km_ref, kx_ref)], axis=0) for kv in range(2)]
        KT = K.T

        zero = jnp.zeros((112, 128), f32)

        def rows16(ref):
            x = ref[...].astype(f32)
            return jnp.concatenate([x[:, n * 1024 + g * 128 : n * 1024 + g * 128 + 128] for g in range(8)] + [zero], axis=0)

        pq, pg, po = rows16(pq_ref), rows16(pg_ref), rows16(po_ref)
        delta = row_delta(pg, po)[0:1]
        pq, pg = pq.astype(bf), pg.astype(bf)
        Q = jnp.concatenate([qs_ref[n], pq], axis=0)
        G = jnp.concatenate([gs_ref[n], pg], axis=0)
        low = jnp.full((1, 128), NEG, f32)
        m_own = jnp.concatenate([st_ref[n, 0:1], low], axis=1)
        l_own = jnp.concatenate([st_ref[n, 8:9], jnp.zeros((1, 128), f32)], axis=1)
        both_delta = jnp.concatenate([dl_ref[n, 0:1], delta], axis=1)
        S = dot_t(K, Q) + jnp.concatenate([bias_ref[...]] * 8 + [pbias_ref[...]], axis=1)
        m = jnp.maximum(jnp.max(S, axis=0, keepdims=True) * C2, m_own)
        e = jnp.exp2(S * C2 - m)
        total = jnp.sum(e, axis=0, keepdims=True) + l_own * jnp.exp2(m_own - m)
        lse_ref[n] = jnp.broadcast_to((m + jnp.log2(total))[:, 0:1024], (8, 1024))
        p = e * (1.0 / total)
        ds = (p * (dot_t(V, G) - both_delta)).astype(bf)
        dv = dot(p.astype(bf), G)
        dk = dot(ds, Q)
        dq = dot(KT, ds)
        dqt_ref[n] = dq[:, 0:1024]
        pdq = dq[:, 1024:1152].T * SCALE
        for g in range(8):
            pdq_ref[:, n * 1024 + g * 128 : n * 1024 + g * 128 + 128] = pdq[2 * g : 2 * g + 2].astype(bf)

        for side in range(2):
            s = slice(256 * side, 256 * side + 256)
            d_ref[:, side, 2 * n] = (dk[s] * SCALE).astype(bf).reshape(8, 32, 128)
            d_ref[:, side, 2 * n + 1] = dv[s].astype(bf).reshape(8, 32, 128)


def own_grads_kernel(CH, qs_ref, gs_ref, dl_ref, lse_ref, dqt_ref, k_ref, v_ref, dq_ref, d_ref, bias_ref, dk_ref, dv_ref):
    @pl.when(pl.program_id(0) == 0)
    def _():
        bias_ref[...] = causal_bias(lax.axis_index("ctx"))

    K, V = k_ref[...].reshape(1024, 128), v_ref[...].reshape(1024, 128)
    KT = K.T
    dk_ref[...] = jnp.zeros((1024, 128), f32)
    dv_ref[...] = jnp.zeros((1024, 128), f32)

    @pl.loop(0, 1024 // CH)
    def _(i):
        rows = pl.ds(pl.multiple_of(i * CH, CH), CH)
        Q, G = qs_ref[0, rows], gs_ref[0, rows]
        S = dot_t(K, Q) + jnp.concatenate([bias_ref[...]] * (CH // 128), axis=1)
        p = jnp.exp2(S * C2 - lse_ref[0, 0:1, rows])
        ds = (p * (dot_t(V, G) - dl_ref[0, 0:1, rows])).astype(bf)
        dv_ref[...] += dot(p.astype(bf), G)
        dk_ref[...] += dot(ds, Q)
        dq = ((dqt_ref[0, :, rows] + dot(KT, ds)) * SCALE).T
        for j in range(CH // 128):
            lanes = pl.ds(pl.multiple_of(i * CH + j * 128, 128), 128)
            dq_ref[:, lanes] = dq[j * 128 : j * 128 + 128].astype(bf)

    d_ref[:, 0:128] = (dk_ref[...] * SCALE).astype(bf).reshape(8, 128, 128)
    d_ref[:, 128:256] = dv_ref[...].astype(bf).reshape(8, 128, 128)


SMEM = pl.BlockSpec(memory_space=pltpu.SMEM)


def wide(n):
    return pl.BlockSpec((n, 1024), lambda h: (0, h))


def per_head(*shape):
    return pl.BlockSpec((1,) + shape, lambda h: (h, 0, 0))


def own_block(kv):
    return pl.BlockSpec((8, 128, 128), lambda h: (0, 2 * h + kv, 0))


def shape_of(*shape, dtype=bf):
    return jax.ShapeDtypeStruct(shape, dtype)


def cost(gflops, megabytes):
    return pl.CostEstimate(flops=int(gflops * 1e9), bytes_accessed=int(megabytes * 2**20), transcendentals=0)


def prepare(length, q, g, o):
    return pl.pallas_call(
        prepare_kernel,
        grid=(4,),
        in_specs=[SMEM, wide(128), wide(128), wide(128)],
        out_specs=[per_head(1024, 128), per_head(1024, 128), per_head(8, 1024)],
        out_shape=[shape_of(4, 1024, 128), shape_of(4, 1024, 128), shape_of(4, 8, 1024, dtype=f32)],
        compiler_params=LIMIT,
        cost_estimate=cost(0.1, 5),
    )(length, q, g, o)


def own_stats(qs, own):
    return pl.pallas_call(
        own_stats_kernel,
        grid=(4,),
        in_specs=[per_head(1024, 128), own_block(0)],
        out_specs=per_head(16, 1024),
        out_shape=shape_of(4, 16, 1024, dtype=f32),
        scratch_shapes=[pltpu.VMEM((1024, 128), f32)],
        compiler_params=LIMIT,
        cost_estimate=cost(1.2, 6),
    )(qs, own)


def prefix(prompt, offset, qs, gs, st, delta, mine, other, pq, pg, po, HP=1):
    def heads(*shape):
        return pl.BlockSpec((HP,) + shape, lambda h: (h, 0, 0))

    big = pl.BlockSpec((8, 2 * HP, 32, 128), lambda h: (0, h, 0, 0))
    row = pl.BlockSpec((2, 1024 * HP), lambda h: (0, h))
    return pl.pallas_call(
        functools.partial(prefix_kernel, HP),
        grid=(4 // HP,),
        in_specs=[SMEM, SMEM, heads(1024, 128), heads(1024, 128), heads(16, 1024), heads(8, 1024), big, big, row, row, row],
        out_specs=[pl.BlockSpec((8, 2, 2 * HP, 32, 128), lambda h: (0, 0, h, 0, 0)), heads(128, 1024), heads(8, 1024), row],
        out_shape=[shape_of(8, 2, 8, 32, 128), shape_of(4, 128, 1024, dtype=f32),
                   shape_of(4, 8, 1024, dtype=f32), shape_of(2, 4096)],
        scratch_shapes=[pltpu.VMEM((512, 128), f32), pltpu.VMEM((512, 128), f32)],
        compiler_params=LIMIT,
        cost_estimate=cost(2.7, 8),
    )(prompt, offset, qs, gs, st, delta, mine, other, pq, pg, po)


def own_grads(qs, gs, delta, lse, dqt, own, CH=1024):
    return pl.pallas_call(
        functools.partial(own_grads_kernel, CH),
        grid=(4,),
        in_specs=[per_head(1024, 128), per_head(1024, 128), per_head(8, 1024), per_head(8, 1024), per_head(128, 1024),
                  own_block(0), own_block(1)],
        out_specs=[wide(128), pl.BlockSpec((8, 256, 128), lambda h: (0, h, 0))],
        out_shape=[shape_of(128, 4096), shape_of(8, 1024, 128)],
        scratch_shapes=[pltpu.VMEM((1024, 128), f32)] * 3,
        compiler_params=LIMIT,
        cost_estimate=cost(5.4, 10),
    )(qs, gs, delta, lse, dqt, own, own)


def copies_kernel(key_ref, value_ref, pack_key_ref, pack_value_ref, out_ref, pack_ref, block, rows, sems):
    taken = [pltpu.make_async_copy(pack_key_ref, rows.at[0], sems.at[16]), pltpu.make_async_copy(pack_value_ref, rows.at[1], sems.at[17])]
    for h in range(4):
        for kv, ref in enumerate((key_ref, value_ref)):
            i = 2 * h + kv
            source = ref.at[:, pl.ds(h * 128, 128)]
            taken.append(pltpu.make_async_copy(source, block.at[pl.ds(i * 128, 128)], sems.at[8 + i]))
    for copy in taken:
        copy.start()
    for copy in taken:
        copy.wait()
    sent = [pltpu.make_async_copy(block, out_ref.at[i], sems.at[i]) for i in range(8)]
    for copy in sent:
        copy.start()
    both = rows[...].astype(f32)
    parts = [both[kv][:, h * 128 : h * 128 + 128] for h in range(4) for kv in range(2)]
    pack_ref[...] = jnp.concatenate(parts, axis=0).astype(bf)
    for copy in sent:
        copy.wait()


def copies_of(key, value, pack_key, pack_value):
    return pl.pallas_call(
        copies_kernel,
        in_specs=[pl.BlockSpec(memory_space=pltpu.HBM)] * 4,
        out_specs=[pl.BlockSpec(memory_space=pl.ANY), pl.BlockSpec(memory_space=pltpu.VMEM)],
        out_shape=[shape_of(8, 1024, 128), shape_of(16, 128)],
        scratch_shapes=[pltpu.VMEM((1024, 128), bf), pltpu.VMEM((2, 2, 512), bf), pltpu.SemaphoreType.DMA((18,))],
        compiler_params=LIMIT,
        cost_estimate=cost(0, 2),
    )(key, value, pack_key, pack_value)


def regroup_kernel(*refs):
    x = jnp.concatenate([ref[...].astype(f32) for ref in refs[:-1]], axis=0)
    for k in range(8):
        rows = [x[16 * i + 2 * k : 16 * i + 2 * k + 2] for i in range(16)]
        rows = jnp.concatenate(rows, axis=0).astype(bf)
        for c in range(8):
            refs[-1][c, k] = rows


def regroup(*blocks):
    return pl.pallas_call(
        regroup_kernel,
        out_shape=shape_of(8, 8, 32, 128),
        compiler_params=SMALL,
        cost_estimate=cost(0, 1),
    )(*blocks)


def ungroup_kernel(parts_ref, *refs):
    total = jnp.sum(parts_ref[...].astype(f32), axis=0)
    for m in range(4):
        rows = [total[s, k, 8 * i + 2 * m : 8 * i + 2 * m + 2] for s in range(2) for i in range(4) for k in range(8)]
        refs[m][...] = jnp.concatenate(rows, axis=0).astype(bf)


def ungroup(parts):
    return pl.pallas_call(
        ungroup_kernel,
        out_shape=[shape_of(128, 128)] * 4,
        compiler_params=SMALL,
        cost_estimate=cost(0, 1),
    )(parts)


def quarter_kernel(*refs):
    total = sum(ref[...].astype(f32) for ref in refs[:4])
    for m in range(4):
        both = [total[i : i + 16] for i in (16 * m, 64 + 16 * m)]
        refs[4 + m][...] = jnp.concatenate(both, axis=0).astype(bf)


def quarter(*blocks):
    return pl.pallas_call(
        quarter_kernel,
        out_shape=[shape_of(32, 128)] * 4,
        compiler_params=SMALL,
        cost_estimate=cost(0, 0.1),
    )(*blocks)


def sides_kernel(a_ref, b_ref, c_ref, d_ref, mine_ref, other_ref):
    total = sum(ref[...].astype(f32) for ref in (a_ref, b_ref, c_ref, d_ref))
    mine_ref[...] = total[0:16].astype(bf)
    other_ref[...] = total[16:32].astype(bf)


def sides(*blocks):
    return pl.pallas_call(
        sides_kernel, out_shape=[shape_of(16, 128)] * 2, compiler_params=SMALL, cost_estimate=cost(0, 0.1)
    )(*blocks)


def finish_pack_kernel(a_ref, b_ref, key_ref, value_ref):
    rows = a_ref[...].astype(f32) + b_ref[...].astype(f32)
    key_ref[...] = jnp.concatenate([rows[4 * h : 4 * h + 2] for h in range(4)], axis=1).astype(bf)
    value_ref[...] = jnp.concatenate([rows[4 * h + 2 : 4 * h + 4] for h in range(4)], axis=1).astype(bf)


def finish_pack(*blocks):
    return pl.pallas_call(
        finish_pack_kernel, out_shape=[shape_of(2, 512)] * 2, compiler_params=SMALL, cost_estimate=cost(0, 0.1)
    )(*blocks)


def finish_own_kernel(parts_ref, key_ref, value_ref):
    total = jnp.sum(parts_ref[...].astype(f32), axis=0)
    key_ref[...] = total[0:128].astype(bf)
    value_ref[...] = total[128:256].astype(bf)


def finish_own(parts):
    column = pl.BlockSpec((128, 128), lambda h: (0, h))
    return pl.pallas_call(
        finish_own_kernel,
        grid=(4,),
        in_specs=[pl.BlockSpec((8, 256, 128), lambda h: (0, h, 0))],
        out_specs=[column, column],
        out_shape=[shape_of(128, 512), shape_of(128, 512)],
        compiler_params=SMALL,
        cost_estimate=cost(0, 3),
    )(parts)


def from_partner(block, mask):
    return lax.ppermute(block, "resp", [(i, i ^ mask) for i in range(32)])


def exchange(blocks):
    return lax.all_to_all(blocks, "ctx", 0, 0, tiled=True)


def shards(
    resp_query, resp_key, resp_value, resp_out, resp_grad,
    pack_query, pack_key, pack_value, pack_out, pack_grad,
    resp_length, prompt_id, pack_offset,
):
    copies, block = copies_of(resp_key[0], resp_value[0], pack_key, pack_value)
    own = exchange(copies)
    for mask in (2, 4, 8):
        block = jnp.concatenate([block, from_partner(block, mask)], axis=0)
    block, q, g, o = lax.optimization_barrier((block, resp_query[0], resp_grad[0], resp_out[0]))
    qs, gs, delta = prepare(resp_length, q, g, o)
    last, qs = lax.optimization_barrier((from_partner(block, 16), qs))
    mine = exchange(regroup(block, last))
    st = own_stats(qs, own)
    mine, st = lax.optimization_barrier((mine, st))
    other = from_partner(mine, 1)
    d, dqt, lse, pdq = prefix(
        prompt_id, pack_offset, qs, gs, st, delta, mine, other, pack_query, pack_grad, pack_out
    )
    parts = exchange(d)
    dq, down = own_grads(qs, gs, delta, lse, dqt, own)
    parts = ungroup(parts)
    own_parts = exchange(down)
    parts = quarter(parts[0], *[from_partner(parts[m], 2 * m) for m in (1, 2, 3)])
    mine, other = sides(parts[0], *[from_partner(parts[m], 8 * m) for m in (1, 2, 3)])
    block_key, block_value = finish_pack(mine, from_partner(other, 1))
    key, value = finish_own(own_parts)
    return dq[None], key[None], value[None], pdq, block_key, block_value


def solution(mesh):
    long = P("resp", "ctx", None)
    pack = P(("ctx", "resp"), None)
    return jax.shard_map(
        shards,
        mesh=mesh,
        in_specs=(long,) * 5 + (pack,) * 5 + (P("resp"), P("resp"), P()),
        out_specs=(long,) * 3 + (pack,) * 3,
        check_vma=False,
    )
```

```python
import functools
import math

import jax
import jax.numpy as jnp
from jax import lax
from jax.experimental import pallas as pl
from jax.experimental.pallas import tpu as pltpu
from jax.sharding import PartitionSpec as P

bf, f32 = jnp.bfloat16, jnp.float32
SCALE = 128 ** -0.5
C2 = SCALE * math.log2(math.e)
NEG = -1e30
LIMIT = pltpu.CompilerParams(vmem_limit_bytes=60 * 1024 * 1024)
SMALL = pltpu.CompilerParams(vmem_limit_bytes=12 * 1024 * 1024)


def dot_t(a, b):
    return lax.dot_general(a, b, (((1,), (1,)), ((), ())), preferred_element_type=f32)


def dot(a, b):
    return jnp.dot(a, b, preferred_element_type=f32)


def row_delta(grad, out):
    prod = grad * out
    high = prod.astype(bf)
    low = (prod - high.astype(f32)).astype(bf)
    return dot_t(jnp.ones((8, 256), bf), jnp.concatenate([high, low], axis=1))


def causal_bias(ctx):
    u = lax.broadcasted_iota(jnp.int32, (1024, 128), 0)
    r = lax.broadcasted_iota(jnp.int32, (1024, 128), 1)
    return jnp.where(u <= ctx * 128 + r, 0.0, NEG)


def prepare_kernel(len_ref, q_ref, g_ref, o_ref, qs_ref, gs_ref, delta_ref):
    live = len_ref[0] - lax.axis_index("ctx") * 128
    rr = lax.broadcasted_iota(jnp.int32, (128, 128), 0)
    for g in range(8):
        s = slice(g * 128, g * 128 + 128)
        qs_ref[0, s] = q_ref[:, s]
        grad = jnp.where(rr < live, g_ref[:, s].astype(f32), 0.0)
        gs_ref[0, s] = grad.astype(bf)
        delta_ref[0, :, s] = row_delta(grad, o_ref[:, s].astype(f32))


def own_stats_kernel(qs_ref, k_ref, st_ref, bias_ref):
    @pl.when(pl.program_id(0) == 0)
    def _():
        bias_ref[...] = causal_bias(lax.axis_index("ctx"))

    K = k_ref[...].reshape(1024, 128)
    S = dot_t(K, qs_ref[0]) + jnp.concatenate([bias_ref[...]] * 8, axis=1)
    m = jnp.max(S, axis=0, keepdims=True) * C2
    total = jnp.sum(jnp.exp2(S * C2 - m), axis=0, keepdims=True)
    st_ref[0, 0:8] = jnp.broadcast_to(m, (8, 1024))
    st_ref[0, 8:16] = jnp.broadcast_to(total, (8, 1024))


def prefix_kernel(HP, prompt_ref, offset_ref, qs_ref, gs_ref, st_ref, dl_ref, km_ref, kx_ref, pq_ref, pg_ref, po_ref,
                  d_ref, dqt_ref, lse_ref, pdq_ref, bias_ref, pbias_ref):
    resp = lax.axis_index("resp")
    core, row0 = resp & 1, (lax.axis_index("ctx") * 32 + resp) * 2
    split = offset_ref[1]
    lo = jnp.where(prompt_ref[0] == 0, 0, split)
    hi = jnp.where(prompt_ref[0] == 0, split, 512)

    @pl.when(pl.program_id(0) == 0)
    def _():
        i = lax.broadcasted_iota(jnp.int32, (512, 128), 0)
        side, j = i >> 8, i & 255
        pos = (j >> 5) * 64 + ((resp >> 1) ^ ((j >> 1) & 15)) * 4 + (core ^ side) * 2 + (j & 1)
        bias_ref[...] = jnp.where((pos >= lo) & (pos < hi), 0.0, NEG)
        prow = row0 + (lax.broadcasted_iota(jnp.int32, (512, 128), 1) & 1)
        seen = (pos <= prow) & ((pos >= split) == (prow >= split))
        pbias_ref[...] = jnp.where(seen, 0.0, NEG)

    for n in range(HP):
        K, V = [jnp.concatenate([ref[:, 2 * n + kv].reshape(256, 128) for ref in (km_ref, kx_ref)], axis=0) for kv in range(2)]
        KT = K.T

        zero = jnp.zeros((112, 128), f32)

        def rows16(ref):
            x = ref[...].astype(f32)
            return jnp.concatenate([x[:, n * 1024 + g * 128 : n * 1024 + g * 128 + 128] for g in range(8)] + [zero], axis=0)

        pq, pg, po = rows16(pq_ref), rows16(pg_ref), rows16(po_ref)
        delta = row_delta(pg, po)[0:1]
        pq, pg = pq.astype(bf), pg.astype(bf)
        Q = jnp.concatenate([qs_ref[n], pq], axis=0)
        G = jnp.concatenate([gs_ref[n], pg], axis=0)
        low = jnp.full((1, 128), NEG, f32)
        m_own = jnp.concatenate([st_ref[n, 0:1], low], axis=1)
        l_own = jnp.concatenate([st_ref[n, 8:9], jnp.zeros((1, 128), f32)], axis=1)
        both_delta = jnp.concatenate([dl_ref[n, 0:1], delta], axis=1)
        S = dot_t(K, Q) + jnp.concatenate([bias_ref[...]] * 8 + [pbias_ref[...]], axis=1)
        m = jnp.maximum(jnp.max(S, axis=0, keepdims=True) * C2, m_own)
        e = jnp.exp2(S * C2 - m)
        total = jnp.sum(e, axis=0, keepdims=True) + l_own * jnp.exp2(m_own - m)
        lse_ref[n] = jnp.broadcast_to((m + jnp.log2(total))[:, 0:1024], (8, 1024))
        p = e * (1.0 / total)
        ds = (p * (dot_t(V, G) - both_delta)).astype(bf)
        dv = dot(p.astype(bf), G)
        dk = dot(ds, Q)
        dq = dot(KT, ds)
        dqt_ref[n] = dq[:, 0:1024]
        pdq = dq[:, 1024:1152].T * SCALE
        for g in range(8):
            pdq_ref[:, n * 1024 + g * 128 : n * 1024 + g * 128 + 128] = pdq[2 * g : 2 * g + 2].astype(bf)

        for side in range(2):
            s = slice(256 * side, 256 * side + 256)
            d_ref[:, side, 2 * n] = (dk[s] * SCALE).astype(bf).reshape(8, 32, 128)
            d_ref[:, side, 2 * n + 1] = dv[s].astype(bf).reshape(8, 32, 128)


def own_grads_kernel(CH, qs_ref, gs_ref, dl_ref, lse_ref, dqt_ref, k_ref, v_ref, dq_ref, d_ref, bias_ref, dk_ref, dv_ref):
    @pl.when(pl.program_id(0) == 0)
    def _():
        bias_ref[...] = causal_bias(lax.axis_index("ctx"))

    K, V = k_ref[...].reshape(1024, 128), v_ref[...].reshape(1024, 128)
    KT = K.T
    dk_ref[...] = jnp.zeros((1024, 128), f32)
    dv_ref[...] = jnp.zeros((1024, 128), f32)

    @pl.loop(0, 1024 // CH)
    def _(i):
        rows = pl.ds(pl.multiple_of(i * CH, CH), CH)
        Q, G = qs_ref[0, rows], gs_ref[0, rows]
        S = dot_t(K, Q) + jnp.concatenate([bias_ref[...]] * (CH // 128), axis=1)
        p = jnp.exp2(S * C2 - lse_ref[0, 0:1, rows])
        ds = (p * (dot_t(V, G) - dl_ref[0, 0:1, rows])).astype(bf)
        dv_ref[...] += dot(p.astype(bf), G)
        dk_ref[...] += dot(ds, Q)
        dq = ((dqt_ref[0, :, rows] + dot(KT, ds)) * SCALE).T
        for j in range(CH // 128):
            lanes = pl.ds(pl.multiple_of(i * CH + j * 128, 128), 128)
            dq_ref[:, lanes] = dq[j * 128 : j * 128 + 128].astype(bf)

    d_ref[:, 0:128] = (dk_ref[...] * SCALE).astype(bf).reshape(8, 128, 128)
    d_ref[:, 128:256] = dv_ref[...].astype(bf).reshape(8, 128, 128)


SMEM = pl.BlockSpec(memory_space=pltpu.SMEM)


def wide(n):
    return pl.BlockSpec((n, 1024), lambda h: (0, h))


def per_head(*shape):
    return pl.BlockSpec((1,) + shape, lambda h: (h, 0, 0))


def own_block(kv):
    return pl.BlockSpec((8, 128, 128), lambda h: (0, 2 * h + kv, 0))


def shape_of(*shape, dtype=bf):
    return jax.ShapeDtypeStruct(shape, dtype)


def cost(gflops, megabytes):
    return pl.CostEstimate(flops=int(gflops * 1e9), bytes_accessed=int(megabytes * 2**20), transcendentals=0)


def prepare(length, q, g, o):
    return pl.pallas_call(
        prepare_kernel,
        grid=(4,),
        in_specs=[SMEM, wide(128), wide(128), wide(128)],
        out_specs=[per_head(1024, 128), per_head(1024, 128), per_head(8, 1024)],
        out_shape=[shape_of(4, 1024, 128), shape_of(4, 1024, 128), shape_of(4, 8, 1024, dtype=f32)],
        compiler_params=LIMIT,
        cost_estimate=cost(0.1, 5),
    )(length, q, g, o)


def own_stats(qs, own):
    return pl.pallas_call(
        own_stats_kernel,
        grid=(4,),
        in_specs=[per_head(1024, 128), own_block(0)],
        out_specs=per_head(16, 1024),
        out_shape=shape_of(4, 16, 1024, dtype=f32),
        scratch_shapes=[pltpu.VMEM((1024, 128), f32)],
        compiler_params=LIMIT,
        cost_estimate=cost(1.2, 6),
    )(qs, own)


def prefix(prompt, offset, qs, gs, st, delta, mine, other, pq, pg, po, HP=1):
    def heads(*shape):
        return pl.BlockSpec((HP,) + shape, lambda h: (h, 0, 0))

    big = pl.BlockSpec((8, 2 * HP, 32, 128), lambda h: (0, h, 0, 0))
    row = pl.BlockSpec((2, 1024 * HP), lambda h: (0, h))
    return pl.pallas_call(
        functools.partial(prefix_kernel, HP),
        grid=(4 // HP,),
        in_specs=[SMEM, SMEM, heads(1024, 128), heads(1024, 128), heads(16, 1024), heads(8, 1024), big, big, row, row, row],
        out_specs=[pl.BlockSpec((8, 2, 2 * HP, 32, 128), lambda h: (0, 0, h, 0, 0)), heads(128, 1024), heads(8, 1024), row],
        out_shape=[shape_of(8, 2, 8, 32, 128), shape_of(4, 128, 1024, dtype=f32),
                   shape_of(4, 8, 1024, dtype=f32), shape_of(2, 4096)],
        scratch_shapes=[pltpu.VMEM((512, 128), f32), pltpu.VMEM((512, 128), f32)],
        compiler_params=LIMIT,
        cost_estimate=cost(2.7, 8),
    )(prompt, offset, qs, gs, st, delta, mine, other, pq, pg, po)


def own_grads(qs, gs, delta, lse, dqt, own, CH=1024):
    return pl.pallas_call(
        functools.partial(own_grads_kernel, CH),
        grid=(4,),
        in_specs=[per_head(1024, 128), per_head(1024, 128), per_head(8, 1024), per_head(8, 1024), per_head(128, 1024),
                  own_block(0), own_block(1)],
        out_specs=[wide(128), pl.BlockSpec((8, 256, 128), lambda h: (0, h, 0))],
        out_shape=[shape_of(128, 4096), shape_of(8, 1024, 128)],
        scratch_shapes=[pltpu.VMEM((1024, 128), f32)] * 3,
        compiler_params=LIMIT,
        cost_estimate=cost(5.4, 10),
    )(qs, gs, delta, lse, dqt, own, own)


def copies_kernel(key_ref, value_ref, pack_key_ref, pack_value_ref, out_ref, pack_ref, block, rows, sems):
    taken = [pltpu.make_async_copy(pack_key_ref, rows.at[0], sems.at[16]), pltpu.make_async_copy(pack_value_ref, rows.at[1], sems.at[17])]
    for h in range(4):
        for kv, ref in enumerate((key_ref, value_ref)):
            i = 2 * h + kv
            source = ref.at[:, pl.ds(h * 128, 128)]
            taken.append(pltpu.make_async_copy(source, block.at[pl.ds(i * 128, 128)], sems.at[8 + i]))
    for copy in taken:
        copy.start()
    for copy in taken:
        copy.wait()
    sent = [pltpu.make_async_copy(block, out_ref.at[i], sems.at[i]) for i in range(8)]
    for copy in sent:
        copy.start()
    both = rows[...].astype(f32)
    parts = [both[kv][:, h * 128 : h * 128 + 128] for h in range(4) for kv in range(2)]
    pack_ref[...] = jnp.concatenate(parts, axis=0).astype(bf)
    for copy in sent:
        copy.wait()


def copies_of(key, value, pack_key, pack_value):
    return pl.pallas_call(
        copies_kernel,
        in_specs=[pl.BlockSpec(memory_space=pltpu.HBM)] * 4,
        out_specs=[pl.BlockSpec(memory_space=pl.ANY), pl.BlockSpec(memory_space=pltpu.VMEM)],
        out_shape=[shape_of(8, 1024, 128), shape_of(16, 128)],
        scratch_shapes=[pltpu.VMEM((1024, 128), bf), pltpu.VMEM((2, 2, 512), bf), pltpu.SemaphoreType.DMA((18,))],
        compiler_params=LIMIT,
        cost_estimate=cost(0, 2),
    )(key, value, pack_key, pack_value)


def regroup_kernel(*refs):
    x = jnp.concatenate([ref[...].astype(f32) for ref in refs[:-1]], axis=0)
    for k in range(8):
        rows = [x[16 * i + 2 * k : 16 * i + 2 * k + 2] for i in range(16)]
        rows = jnp.concatenate(rows, axis=0).astype(bf)
        for c in range(8):
            refs[-1][c, k] = rows


def regroup(*blocks):
    return pl.pallas_call(
        regroup_kernel,
        out_shape=shape_of(8, 8, 32, 128),
        compiler_params=SMALL,
        cost_estimate=cost(0, 1),
    )(*blocks)


def ungroup_kernel(parts_ref, keep_ref, away_ref):
    total = jnp.sum(parts_ref[...].astype(f32), axis=0)
    for b, ref in enumerate((keep_ref, away_ref)):
        rows = [
            total[s, k, 8 * i + 4 * c + 2 * b : 8 * i + 4 * c + 2 * b + 2]
            for c in range(2) for s in range(2) for i in range(4) for k in range(8)
        ]
        ref[...] = jnp.concatenate(rows, axis=0).astype(bf)


def ungroup(parts):
    return pl.pallas_call(
        ungroup_kernel,
        out_shape=[shape_of(256, 128)] * 2,
        compiler_params=SMALL,
        cost_estimate=cost(0, 1),
    )(parts)


def halve_kernel(a_ref, b_ref, keep_ref, away_ref):
    total = a_ref[...].astype(f32) + b_ref[...].astype(f32)
    keep_ref[...] = total[0:128].astype(bf)
    away_ref[...] = total[128:256].astype(bf)


def halve(*blocks):
    return pl.pallas_call(
        halve_kernel, out_shape=[shape_of(128, 128)] * 2, compiler_params=SMALL, cost_estimate=cost(0, 0.1)
    )(*blocks)


def quarter_kernel(a_ref, b_ref, *refs):
    total = a_ref[...].astype(f32) + b_ref[...].astype(f32)
    for m in range(4):
        both = [total[i : i + 16] for i in (16 * m, 64 + 16 * m)]
        refs[m][...] = jnp.concatenate(both, axis=0).astype(bf)


def quarter(*blocks):
    return pl.pallas_call(
        quarter_kernel, out_shape=[shape_of(32, 128)] * 4, compiler_params=SMALL, cost_estimate=cost(0, 0.1)
    )(*blocks)


def sides_kernel(a_ref, b_ref, c_ref, d_ref, mine_ref, other_ref):
    total = sum(ref[...].astype(f32) for ref in (a_ref, b_ref, c_ref, d_ref))
    mine_ref[...] = total[0:16].astype(bf)
    other_ref[...] = total[16:32].astype(bf)


def sides(*blocks):
    return pl.pallas_call(
        sides_kernel, out_shape=[shape_of(16, 128)] * 2, compiler_params=SMALL, cost_estimate=cost(0, 0.1)
    )(*blocks)


def finish_pack_kernel(a_ref, b_ref, key_ref, value_ref):
    rows = a_ref[...].astype(f32) + b_ref[...].astype(f32)
    key_ref[...] = jnp.concatenate([rows[4 * h : 4 * h + 2] for h in range(4)], axis=1).astype(bf)
    value_ref[...] = jnp.concatenate([rows[4 * h + 2 : 4 * h + 4] for h in range(4)], axis=1).astype(bf)


def finish_pack(*blocks):
    return pl.pallas_call(
        finish_pack_kernel, out_shape=[shape_of(2, 512)] * 2, compiler_params=SMALL, cost_estimate=cost(0, 0.1)
    )(*blocks)


def finish_own_kernel(parts_ref, key_ref, value_ref):
    total = jnp.sum(parts_ref[...].astype(f32), axis=0)
    key_ref[...] = total[0:128].astype(bf)
    value_ref[...] = total[128:256].astype(bf)


def finish_own(parts):
    column = pl.BlockSpec((128, 128), lambda h: (0, h))
    return pl.pallas_call(
        finish_own_kernel,
        grid=(4,),
        in_specs=[pl.BlockSpec((8, 256, 128), lambda h: (0, h, 0))],
        out_specs=[column, column],
        out_shape=[shape_of(128, 512), shape_of(128, 512)],
        compiler_params=SMALL,
        cost_estimate=cost(0, 3),
    )(parts)


def from_partner(block, mask):
    return lax.ppermute(block, "resp", [(i, i ^ mask) for i in range(32)])


def exchange(blocks):
    return lax.all_to_all(blocks, "ctx", 0, 0, tiled=True)


def shards(
    resp_query, resp_key, resp_value, resp_out, resp_grad,
    pack_query, pack_key, pack_value, pack_out, pack_grad,
    resp_length, prompt_id, pack_offset,
):
    copies, block = copies_of(resp_key[0], resp_value[0], pack_key, pack_value)
    own = exchange(copies)
    for mask in (2, 4, 8):
        block = jnp.concatenate([block, from_partner(block, mask)], axis=0)
    block, q, g, o = lax.optimization_barrier((block, resp_query[0], resp_grad[0], resp_out[0]))
    qs, gs, delta = prepare(resp_length, q, g, o)
    last, qs = lax.optimization_barrier((from_partner(block, 16), qs))
    mine = exchange(regroup(block, last))
    st = own_stats(qs, own)
    mine, st = lax.optimization_barrier((mine, st))
    other = from_partner(mine, 1)
    d, dqt, lse, pdq = prefix(
        prompt_id, pack_offset, qs, gs, st, delta, mine, other, pack_query, pack_grad, pack_out
    )
    parts = exchange(d)
    dq, down = own_grads(qs, gs, delta, lse, dqt, own)
    keep, away = ungroup(parts)
    own_parts = exchange(down)
    keep, away = halve(keep, from_partner(away, 2))
    parts = quarter(keep, from_partner(away, 4))
    mine, other = sides(parts[0], *[from_partner(parts[m], 8 * m) for m in (1, 2, 3)])
    key, value = finish_own(own_parts)
    mine, key = lax.optimization_barrier((mine, key))
    block_key, block_value = finish_pack(mine, from_partner(other, 1))
    return dq[None], key[None], value[None], pdq, block_key, block_value


def solution(mesh):
    long = P("resp", "ctx", None)
    pack = P(("ctx", "resp"), None)
    return jax.shard_map(
        shards,
        mesh=mesh,
        in_specs=(long,) * 5 + (pack,) * 5 + (P("resp"), P("resp"), P()),
        out_specs=(long,) * 3 + (pack,) * 3,
        check_vma=False,
    )
```

```python
import functools
import math

import jax
import jax.numpy as jnp
from jax import lax
from jax.experimental import pallas as pl
from jax.experimental.pallas import tpu as pltpu
from jax.sharding import PartitionSpec as P

bf, f32 = jnp.bfloat16, jnp.float32
SCALE = 128 ** -0.5
C2 = SCALE * math.log2(math.e)
NEG = -1e30
LIMIT = pltpu.CompilerParams(vmem_limit_bytes=60 * 1024 * 1024)
SMALL = pltpu.CompilerParams(vmem_limit_bytes=12 * 1024 * 1024)


def dot_t(a, b):
    return lax.dot_general(a, b, (((1,), (1,)), ((), ())), preferred_element_type=f32)


def dot(a, b):
    return jnp.dot(a, b, preferred_element_type=f32)


def row_delta(grad, out):
    prod = grad * out
    high = prod.astype(bf)
    low = (prod - high.astype(f32)).astype(bf)
    return dot_t(jnp.ones((8, 256), bf), jnp.concatenate([high, low], axis=1))


def causal_bias(ctx):
    u = lax.broadcasted_iota(jnp.int32, (1024, 128), 0)
    r = lax.broadcasted_iota(jnp.int32, (1024, 128), 1)
    return jnp.where(u <= ctx * 128 + r, 0.0, NEG)


def prepare_kernel(len_ref, q_ref, g_ref, o_ref, qs_ref, gs_ref, delta_ref):
    live = len_ref[0] - lax.axis_index("ctx") * 128
    rr = lax.broadcasted_iota(jnp.int32, (128, 128), 0)
    for g in range(8):
        s = slice(g * 128, g * 128 + 128)
        qs_ref[0, s] = q_ref[:, s]
        grad = jnp.where(rr < live, g_ref[:, s].astype(f32), 0.0)
        gs_ref[0, s] = grad.astype(bf)
        delta_ref[0, :, s] = row_delta(grad, o_ref[:, s].astype(f32))


def own_stats_kernel(qs_ref, k_ref, st_ref, bias_ref):
    @pl.when(pl.program_id(0) == 0)
    def _():
        bias_ref[...] = causal_bias(lax.axis_index("ctx"))

    K = k_ref[...].reshape(1024, 128)
    S = dot_t(K, qs_ref[0]) + jnp.concatenate([bias_ref[...]] * 8, axis=1)
    m = jnp.max(S, axis=0, keepdims=True) * C2
    total = jnp.sum(jnp.exp2(S * C2 - m), axis=0, keepdims=True)
    st_ref[0, 0:8] = jnp.broadcast_to(m, (8, 1024))
    st_ref[0, 8:16] = jnp.broadcast_to(total, (8, 1024))


def prefix_kernel(HP, prompt_ref, offset_ref, qs_ref, gs_ref, st_ref, dl_ref, km_ref, kx_ref, pq_ref, pg_ref, po_ref,
                  d_ref, dqt_ref, lse_ref, pdq_ref, bias_ref, pbias_ref):
    resp = lax.axis_index("resp")
    core, row0 = resp & 1, (lax.axis_index("ctx") * 32 + resp) * 2
    split = offset_ref[1]
    lo = jnp.where(prompt_ref[0] == 0, 0, split)
    hi = jnp.where(prompt_ref[0] == 0, split, 512)

    @pl.when(pl.program_id(0) == 0)
    def _():
        i = lax.broadcasted_iota(jnp.int32, (512, 128), 0)
        side, j = i >> 8, i & 255
        pos = (j >> 5) * 64 + ((resp >> 1) ^ ((j >> 1) & 15)) * 4 + (core ^ side) * 2 + (j & 1)
        bias_ref[...] = jnp.where((pos >= lo) & (pos < hi), 0.0, NEG)
        prow = row0 + (lax.broadcasted_iota(jnp.int32, (512, 128), 1) & 1)
        seen = (pos <= prow) & ((pos >= split) == (prow >= split))
        pbias_ref[...] = jnp.where(seen, 0.0, NEG)

    for n in range(HP):
        K, V = [jnp.concatenate([ref[:, 2 * n + kv].reshape(256, 128) for ref in (km_ref, kx_ref)], axis=0) for kv in range(2)]
        KT = K.T

        zero = jnp.zeros((112, 128), f32)

        def rows16(ref):
            x = ref[...].astype(f32)
            return jnp.concatenate([x[:, n * 1024 + g * 128 : n * 1024 + g * 128 + 128] for g in range(8)] + [zero], axis=0)

        pq, pg, po = rows16(pq_ref), rows16(pg_ref), rows16(po_ref)
        delta = row_delta(pg, po)[0:1]
        pq, pg = pq.astype(bf), pg.astype(bf)
        Q = jnp.concatenate([qs_ref[n], pq], axis=0)
        G = jnp.concatenate([gs_ref[n], pg], axis=0)
        low = jnp.full((1, 128), NEG, f32)
        m_own = jnp.concatenate([st_ref[n, 0:1], low], axis=1)
        l_own = jnp.concatenate([st_ref[n, 8:9], jnp.zeros((1, 128), f32)], axis=1)
        both_delta = jnp.concatenate([dl_ref[n, 0:1], delta], axis=1)
        S = dot_t(K, Q) + jnp.concatenate([bias_ref[...]] * 8 + [pbias_ref[...]], axis=1)
        m = jnp.maximum(jnp.max(S, axis=0, keepdims=True) * C2, m_own)
        e = jnp.exp2(S * C2 - m)
        total = jnp.sum(e, axis=0, keepdims=True) + l_own * jnp.exp2(m_own - m)
        lse_ref[n] = jnp.broadcast_to((m + jnp.log2(total))[:, 0:1024], (8, 1024))
        p = e * (1.0 / total)
        ds = (p * (dot_t(V, G) - both_delta)).astype(bf)
        dv = dot(p.astype(bf), G)
        dk = dot(ds, Q)
        dq = dot(KT, ds)
        dqt_ref[n] = dq[:, 0:1024]
        pdq = dq[:, 1024:1152].T * SCALE
        for g in range(8):
            pdq_ref[:, n * 1024 + g * 128 : n * 1024 + g * 128 + 128] = pdq[2 * g : 2 * g + 2].astype(bf)

        for side in range(2):
            s = slice(256 * side, 256 * side + 256)
            d_ref[:, side, 2 * n] = (dk[s] * SCALE).astype(bf).reshape(8, 32, 128)
            d_ref[:, side, 2 * n + 1] = dv[s].astype(bf).reshape(8, 32, 128)


def own_grads_kernel(CH, qs_ref, gs_ref, dl_ref, lse_ref, dqt_ref, k_ref, v_ref, dq_ref, d_ref, bias_ref, dk_ref, dv_ref):
    @pl.when(pl.program_id(0) == 0)
    def _():
        bias_ref[...] = causal_bias(lax.axis_index("ctx"))

    K, V = k_ref[...].reshape(1024, 128), v_ref[...].reshape(1024, 128)
    KT = K.T
    dk_ref[...] = jnp.zeros((1024, 128), f32)
    dv_ref[...] = jnp.zeros((1024, 128), f32)

    @pl.loop(0, 1024 // CH)
    def _(i):
        rows = pl.ds(pl.multiple_of(i * CH, CH), CH)
        Q, G = qs_ref[0, rows], gs_ref[0, rows]
        S = dot_t(K, Q) + jnp.concatenate([bias_ref[...]] * (CH // 128), axis=1)
        p = jnp.exp2(S * C2 - lse_ref[0, 0:1, rows])
        ds = (p * (dot_t(V, G) - dl_ref[0, 0:1, rows])).astype(bf)
        dv_ref[...] += dot(p.astype(bf), G)
        dk_ref[...] += dot(ds, Q)
        dq = ((dqt_ref[0, :, rows] + dot(KT, ds)) * SCALE).T
        for j in range(CH // 128):
            lanes = pl.ds(pl.multiple_of(i * CH + j * 128, 128), 128)
            dq_ref[:, lanes] = dq[j * 128 : j * 128 + 128].astype(bf)

    d_ref[:, 0:128] = (dk_ref[...] * SCALE).astype(bf).reshape(8, 128, 128)
    d_ref[:, 128:256] = dv_ref[...].astype(bf).reshape(8, 128, 128)


SMEM = pl.BlockSpec(memory_space=pltpu.SMEM)


def wide(n):
    return pl.BlockSpec((n, 1024), lambda h: (0, h))


def per_head(*shape):
    return pl.BlockSpec((1,) + shape, lambda h: (h, 0, 0))


def own_block(kv):
    return pl.BlockSpec((8, 128, 128), lambda h: (0, 2 * h + kv, 0))


def shape_of(*shape, dtype=bf):
    return jax.ShapeDtypeStruct(shape, dtype)


def cost(gflops, megabytes):
    return pl.CostEstimate(flops=int(gflops * 1e9), bytes_accessed=int(megabytes * 2**20), transcendentals=0)


def prepare(length, q, g, o):
    return pl.pallas_call(
        prepare_kernel,
        grid=(4,),
        in_specs=[SMEM, wide(128), wide(128), wide(128)],
        out_specs=[per_head(1024, 128), per_head(1024, 128), per_head(8, 1024)],
        out_shape=[shape_of(4, 1024, 128), shape_of(4, 1024, 128), shape_of(4, 8, 1024, dtype=f32)],
        compiler_params=LIMIT,
        cost_estimate=cost(0.1, 5),
    )(length, q, g, o)


def own_stats(qs, own):
    return pl.pallas_call(
        own_stats_kernel,
        grid=(4,),
        in_specs=[per_head(1024, 128), own_block(0)],
        out_specs=per_head(16, 1024),
        out_shape=shape_of(4, 16, 1024, dtype=f32),
        scratch_shapes=[pltpu.VMEM((1024, 128), f32)],
        compiler_params=LIMIT,
        cost_estimate=cost(1.2, 6),
    )(qs, own)


def prefix(prompt, offset, qs, gs, st, delta, mine, other, pq, pg, po, HP=1):
    def heads(*shape):
        return pl.BlockSpec((HP,) + shape, lambda h: (h, 0, 0))

    big = pl.BlockSpec((8, 2 * HP, 32, 128), lambda h: (0, h, 0, 0))
    row = pl.BlockSpec((2, 1024 * HP), lambda h: (0, h))
    return pl.pallas_call(
        functools.partial(prefix_kernel, HP),
        grid=(4 // HP,),
        in_specs=[SMEM, SMEM, heads(1024, 128), heads(1024, 128), heads(16, 1024), heads(8, 1024), big, big, row, row, row],
        out_specs=[pl.BlockSpec((8, 2, 2 * HP, 32, 128), lambda h: (0, 0, h, 0, 0)), heads(128, 1024), heads(8, 1024), row],
        out_shape=[shape_of(8, 2, 8, 32, 128), shape_of(4, 128, 1024, dtype=f32),
                   shape_of(4, 8, 1024, dtype=f32), shape_of(2, 4096)],
        scratch_shapes=[pltpu.VMEM((512, 128), f32), pltpu.VMEM((512, 128), f32)],
        compiler_params=LIMIT,
        cost_estimate=cost(2.7, 8),
    )(prompt, offset, qs, gs, st, delta, mine, other, pq, pg, po)


def own_grads(qs, gs, delta, lse, dqt, own, CH=1024):
    return pl.pallas_call(
        functools.partial(own_grads_kernel, CH),
        grid=(4,),
        in_specs=[per_head(1024, 128), per_head(1024, 128), per_head(8, 1024), per_head(8, 1024), per_head(128, 1024),
                  own_block(0), own_block(1)],
        out_specs=[wide(128), pl.BlockSpec((8, 256, 128), lambda h: (0, h, 0))],
        out_shape=[shape_of(128, 4096), shape_of(8, 1024, 128)],
        scratch_shapes=[pltpu.VMEM((1024, 128), f32)] * 3,
        compiler_params=LIMIT,
        cost_estimate=cost(5.4, 10),
    )(qs, gs, delta, lse, dqt, own, own)


def copies_kernel(key_ref, value_ref, pack_key_ref, pack_value_ref, out_ref, pack_ref, block, rows, sems):
    taken = [pltpu.make_async_copy(pack_key_ref, rows.at[0], sems.at[16]), pltpu.make_async_copy(pack_value_ref, rows.at[1], sems.at[17])]
    for h in range(4):
        for kv, ref in enumerate((key_ref, value_ref)):
            i = 2 * h + kv
            source = ref.at[:, pl.ds(h * 128, 128)]
            taken.append(pltpu.make_async_copy(source, block.at[pl.ds(i * 128, 128)], sems.at[8 + i]))
    for copy in taken:
        copy.start()
    for copy in taken:
        copy.wait()
    sent = [pltpu.make_async_copy(block, out_ref.at[i], sems.at[i]) for i in range(8)]
    for copy in sent:
        copy.start()
    both = rows[...].astype(f32)
    parts = [both[kv][:, h * 128 : h * 128 + 128] for h in range(4) for kv in range(2)]
    pack_ref[...] = jnp.concatenate(parts, axis=0).astype(bf)
    for copy in sent:
        copy.wait()


def copies_of(key, value, pack_key, pack_value):
    return pl.pallas_call(
        copies_kernel,
        in_specs=[pl.BlockSpec(memory_space=pltpu.HBM)] * 4,
        out_specs=[pl.BlockSpec(memory_space=pl.ANY), pl.BlockSpec(memory_space=pltpu.VMEM)],
        out_shape=[shape_of(8, 1024, 128), shape_of(16, 128)],
        scratch_shapes=[pltpu.VMEM((1024, 128), bf), pltpu.VMEM((2, 2, 512), bf), pltpu.SemaphoreType.DMA((18,))],
        compiler_params=LIMIT,
        cost_estimate=cost(0, 2),
    )(key, value, pack_key, pack_value)


def regroup_kernel(*refs):
    x = jnp.concatenate([ref[...].astype(f32) for ref in refs[:-1]], axis=0)
    for k in range(8):
        rows = [x[16 * i + 2 * k : 16 * i + 2 * k + 2] for i in range(16)]
        rows = jnp.concatenate(rows, axis=0).astype(bf)
        for c in range(8):
            refs[-1][c, k] = rows


def regroup(*blocks):
    return pl.pallas_call(
        regroup_kernel,
        out_shape=shape_of(8, 8, 32, 128),
        compiler_params=SMALL,
        cost_estimate=cost(0, 1),
    )(*blocks)


def ungroup_kernel(parts_ref, *refs):
    total = jnp.sum(parts_ref[...].astype(f32), axis=0)
    for m in range(4):
        rows = [total[s, k, 8 * i + 2 * m : 8 * i + 2 * m + 2] for s in range(2) for i in range(4) for k in range(8)]
        refs[m][...] = jnp.concatenate(rows, axis=0).astype(bf)


def ungroup(parts):
    return pl.pallas_call(
        ungroup_kernel,
        out_shape=[shape_of(128, 128)] * 4,
        compiler_params=SMALL,
        cost_estimate=cost(0, 1),
    )(parts)


def quarter_kernel(*refs):
    total = sum(ref[...].astype(f32) for ref in refs[:4])
    for m in range(4):
        both = [total[i : i + 16] for i in (16 * m, 64 + 16 * m)]
        refs[4 + m][...] = jnp.concatenate(both, axis=0).astype(bf)


def quarter(*blocks):
    return pl.pallas_call(
        quarter_kernel,
        out_shape=[shape_of(32, 128)] * 4,
        compiler_params=SMALL,
        cost_estimate=cost(0, 0.1),
    )(*blocks)


def sides_kernel(a_ref, b_ref, c_ref, d_ref, mine_ref, other_ref):
    total = sum(ref[...].astype(f32) for ref in (a_ref, b_ref, c_ref, d_ref))
    mine_ref[...] = total[0:16].astype(bf)
    other_ref[...] = total[16:32].astype(bf)


def sides(*blocks):
    return pl.pallas_call(
        sides_kernel, out_shape=[shape_of(16, 128)] * 2, compiler_params=SMALL, cost_estimate=cost(0, 0.1)
    )(*blocks)


def finish_pack_kernel(a_ref, b_ref, key_ref, value_ref):
    rows = a_ref[...].astype(f32) + b_ref[...].astype(f32)
    key_ref[...] = jnp.concatenate([rows[4 * h : 4 * h + 2] for h in range(4)], axis=1).astype(bf)
    value_ref[...] = jnp.concatenate([rows[4 * h + 2 : 4 * h + 4] for h in range(4)], axis=1).astype(bf)


def finish_pack(*blocks):
    return pl.pallas_call(
        finish_pack_kernel, out_shape=[shape_of(2, 512)] * 2, compiler_params=SMALL, cost_estimate=cost(0, 0.1)
    )(*blocks)


def finish_own_kernel(parts_ref, key_ref, value_ref):
    total = jnp.sum(parts_ref[...].astype(f32), axis=0)
    key_ref[...] = total[0:128].astype(bf)
    value_ref[...] = total[128:256].astype(bf)


def finish_own(parts):
    column = pl.BlockSpec((128, 128), lambda h: (0, h))
    return pl.pallas_call(
        finish_own_kernel,
        grid=(4,),
        in_specs=[pl.BlockSpec((8, 256, 128), lambda h: (0, h, 0))],
        out_specs=[column, column],
        out_shape=[shape_of(128, 512), shape_of(128, 512)],
        compiler_params=SMALL,
        cost_estimate=cost(0, 3),
    )(parts)


def from_partner(block, mask):
    return lax.ppermute(block, "resp", [(i, i ^ mask) for i in range(32)])


def exchange(blocks):
    return lax.all_to_all(blocks, "ctx", 0, 0, tiled=True)


def shards(
    resp_query, resp_key, resp_value, resp_out, resp_grad,
    pack_query, pack_key, pack_value, pack_out, pack_grad,
    resp_length, prompt_id, pack_offset,
):
    copies, block = copies_of(resp_key[0], resp_value[0], pack_key, pack_value)
    own = exchange(copies)
    for mask in (2, 4, 8):
        block = jnp.concatenate([block, from_partner(block, mask)], axis=0)
    block, q, g, o = lax.optimization_barrier((block, resp_query[0], resp_grad[0], resp_out[0]))
    qs, gs, delta = prepare(resp_length, q, g, o)
    last, qs = lax.optimization_barrier((from_partner(block, 16), qs))
    mine = exchange(regroup(block, last))
    st = own_stats(qs, own)
    mine, st = lax.optimization_barrier((mine, st))
    other = from_partner(mine, 1)
    d, dqt, lse, pdq = prefix(
        prompt_id, pack_offset, qs, gs, st, delta, mine, other, pack_query, pack_grad, pack_out
    )
    parts = exchange(d)
    dq, down = own_grads(qs, gs, delta, lse, dqt, own)
    parts = ungroup(parts)
    own_parts = exchange(down)
    parts = quarter(parts[0], *[from_partner(parts[m], 2 * m) for m in (1, 2, 3)])
    mine, other = sides(parts[0], *[from_partner(parts[m], 8 * m) for m in (1, 2, 3)])
    key, value = finish_own(own_parts)
    mine, key = lax.optimization_barrier((mine, key))
    block_key, block_value = finish_pack(mine, from_partner(other, 1))
    return dq[None], key[None], value[None], pdq, block_key, block_value


def solution(mesh):
    long = P("resp", "ctx", None)
    pack = P(("ctx", "resp"), None)
    return jax.shard_map(
        shards,
        mesh=mesh,
        in_specs=(long,) * 5 + (pack,) * 5 + (P("resp"), P("resp"), P()),
        out_specs=(long,) * 3 + (pack,) * 3,
        check_vma=False,
    )
```

```python
import functools
import math

import jax
import jax.numpy as jnp
from jax import lax
from jax.experimental import pallas as pl
from jax.experimental.pallas import tpu as pltpu
from jax.sharding import PartitionSpec as P

bf, f32 = jnp.bfloat16, jnp.float32
SCALE = 128 ** -0.5
C2 = SCALE * math.log2(math.e)
NEG = -1e30
LIMIT = pltpu.CompilerParams(vmem_limit_bytes=60 * 1024 * 1024)
SMALL = pltpu.CompilerParams(vmem_limit_bytes=12 * 1024 * 1024)


def dot_t(a, b):
    return lax.dot_general(a, b, (((1,), (1,)), ((), ())), preferred_element_type=f32)


def dot(a, b):
    return jnp.dot(a, b, preferred_element_type=f32)


def row_delta(grad, out):
    prod = grad * out
    high = prod.astype(bf)
    low = (prod - high.astype(f32)).astype(bf)
    return dot_t(jnp.ones((8, 256), bf), jnp.concatenate([high, low], axis=1))


def causal_bias(ctx):
    u = lax.broadcasted_iota(jnp.int32, (1024, 128), 0)
    r = lax.broadcasted_iota(jnp.int32, (1024, 128), 1)
    return jnp.where(u <= ctx * 128 + r, 0.0, NEG)


def prepare_kernel(len_ref, q_ref, g_ref, o_ref, qs_ref, gs_ref, delta_ref):
    live = len_ref[0] - lax.axis_index("ctx") * 128
    rr = lax.broadcasted_iota(jnp.int32, (128, 128), 0)
    for g in range(8):
        s = slice(g * 128, g * 128 + 128)
        qs_ref[0, s] = q_ref[:, s]
        grad = jnp.where(rr < live, g_ref[:, s].astype(f32), 0.0)
        gs_ref[0, s] = grad.astype(bf)
        delta_ref[0, :, s] = row_delta(grad, o_ref[:, s].astype(f32))


def own_stats_kernel(qs_ref, k_ref, st_ref, bias_ref):
    @pl.when(pl.program_id(0) == 0)
    def _():
        bias_ref[...] = causal_bias(lax.axis_index("ctx"))

    K = k_ref[...].reshape(1024, 128)
    S = dot_t(K, qs_ref[0]) + jnp.concatenate([bias_ref[...]] * 8, axis=1)
    m = jnp.max(S, axis=0, keepdims=True) * C2
    total = jnp.sum(jnp.exp2(S * C2 - m), axis=0, keepdims=True)
    st_ref[0, 0:8] = jnp.broadcast_to(m, (8, 1024))
    st_ref[0, 8:16] = jnp.broadcast_to(total, (8, 1024))


def prefix_kernel(HP, prompt_ref, offset_ref, qs_ref, gs_ref, st_ref, dl_ref, km_ref, kx_ref, pq_ref, pg_ref, po_ref,
                  d_ref, dqt_ref, lse_ref, pdq_ref, bias_ref, pbias_ref):
    resp = lax.axis_index("resp")
    core, row0 = resp & 1, (lax.axis_index("ctx") * 32 + resp) * 2
    split = offset_ref[1]
    lo = jnp.where(prompt_ref[0] == 0, 0, split)
    hi = jnp.where(prompt_ref[0] == 0, split, 512)

    @pl.when(pl.program_id(0) == 0)
    def _():
        i = lax.broadcasted_iota(jnp.int32, (512, 128), 0)
        side, j = i >> 8, i & 255
        pos = (j >> 5) * 64 + ((resp >> 1) ^ ((j >> 1) & 15)) * 4 + (core ^ side) * 2 + (j & 1)
        bias_ref[...] = jnp.where((pos >= lo) & (pos < hi), 0.0, NEG)
        prow = row0 + (lax.broadcasted_iota(jnp.int32, (512, 128), 1) & 1)
        seen = (pos <= prow) & ((pos >= split) == (prow >= split))
        pbias_ref[...] = jnp.where(seen, 0.0, NEG)

    for n in range(HP):
        K, V = [jnp.concatenate([ref[:, 2 * n + kv].reshape(256, 128) for ref in (km_ref, kx_ref)], axis=0) for kv in range(2)]
        KT = K.T

        zero = jnp.zeros((112, 128), f32)

        def rows16(ref):
            x = ref[...].astype(f32)
            return jnp.concatenate([x[:, n * 1024 + g * 128 : n * 1024 + g * 128 + 128] for g in range(8)] + [zero], axis=0)

        pq, pg, po = rows16(pq_ref), rows16(pg_ref), rows16(po_ref)
        delta = row_delta(pg, po)[0:1]
        pq, pg = pq.astype(bf), pg.astype(bf)
        Q = jnp.concatenate([qs_ref[n], pq], axis=0)
        G = jnp.concatenate([gs_ref[n], pg], axis=0)
        low = jnp.full((1, 128), NEG, f32)
        m_own = jnp.concatenate([st_ref[n, 0:1], low], axis=1)
        l_own = jnp.concatenate([st_ref[n, 8:9], jnp.zeros((1, 128), f32)], axis=1)
        both_delta = jnp.concatenate([dl_ref[n, 0:1], delta], axis=1)
        S = dot_t(K, Q) + jnp.concatenate([bias_ref[...]] * 8 + [pbias_ref[...]], axis=1)
        m = jnp.maximum(jnp.max(S, axis=0, keepdims=True) * C2, m_own)
        e = jnp.exp2(S * C2 - m)
        total = jnp.sum(e, axis=0, keepdims=True) + l_own * jnp.exp2(m_own - m)
        lse_ref[n] = jnp.broadcast_to((m + jnp.log2(total))[:, 0:1024], (8, 1024))
        p = e * (1.0 / total)
        ds = (p * (dot_t(V, G) - both_delta)).astype(bf)
        dv = dot(p.astype(bf), G)
        dk = dot(ds, Q)
        dq = dot(KT, ds)
        dqt_ref[n] = dq[:, 0:1024]
        pdq = dq[:, 1024:1152].T * SCALE
        for g in range(8):
            pdq_ref[:, n * 1024 + g * 128 : n * 1024 + g * 128 + 128] = pdq[2 * g : 2 * g + 2].astype(bf)

        for side in range(2):
            s = slice(256 * side, 256 * side + 256)
            d_ref[:, side, 2 * n] = (dk[s] * SCALE).astype(bf).reshape(8, 32, 128)
            d_ref[:, side, 2 * n + 1] = dv[s].astype(bf).reshape(8, 32, 128)


def own_grads_kernel(CH, qs_ref, gs_ref, dl_ref, lse_ref, dqt_ref, k_ref, v_ref, dq_ref, d_ref, bias_ref, dk_ref, dv_ref):
    @pl.when(pl.program_id(0) == 0)
    def _():
        bias_ref[...] = causal_bias(lax.axis_index("ctx"))

    K, V = k_ref[...].reshape(1024, 128), v_ref[...].reshape(1024, 128)
    KT = K.T
    dk_ref[...] = jnp.zeros((1024, 128), f32)
    dv_ref[...] = jnp.zeros((1024, 128), f32)

    @pl.loop(0, 1024 // CH)
    def _(i):
        rows = pl.ds(pl.multiple_of(i * CH, CH), CH)
        Q, G = qs_ref[0, rows], gs_ref[0, rows]
        S = dot_t(K, Q) + jnp.concatenate([bias_ref[...]] * (CH // 128), axis=1)
        p = jnp.exp2(S * C2 - lse_ref[0, 0:1, rows])
        ds = (p * (dot_t(V, G) - dl_ref[0, 0:1, rows])).astype(bf)
        dv_ref[...] += dot(p.astype(bf), G)
        dk_ref[...] += dot(ds, Q)
        dq = ((dqt_ref[0, :, rows] + dot(KT, ds)) * SCALE).T
        for j in range(CH // 128):
            lanes = pl.ds(pl.multiple_of(i * CH + j * 128, 128), 128)
            dq_ref[:, lanes] = dq[j * 128 : j * 128 + 128].astype(bf)

    d_ref[:, 0:128] = (dk_ref[...] * SCALE).astype(bf).reshape(8, 128, 128)
    d_ref[:, 128:256] = dv_ref[...].astype(bf).reshape(8, 128, 128)


SMEM = pl.BlockSpec(memory_space=pltpu.SMEM)


def wide(n):
    return pl.BlockSpec((n, 1024), lambda h: (0, h))


def per_head(*shape):
    return pl.BlockSpec((1,) + shape, lambda h: (h, 0, 0))


def own_block(kv):
    return pl.BlockSpec((8, 128, 128), lambda h: (0, 2 * h + kv, 0))


def shape_of(*shape, dtype=bf):
    return jax.ShapeDtypeStruct(shape, dtype)


def cost(gflops, megabytes):
    return pl.CostEstimate(flops=int(gflops * 1e9), bytes_accessed=int(megabytes * 2**20), transcendentals=0)


def prepare(length, q, g, o):
    return pl.pallas_call(
        prepare_kernel,
        grid=(4,),
        in_specs=[SMEM, wide(128), wide(128), wide(128)],
        out_specs=[per_head(1024, 128), per_head(1024, 128), per_head(8, 1024)],
        out_shape=[shape_of(4, 1024, 128), shape_of(4, 1024, 128), shape_of(4, 8, 1024, dtype=f32)],
        compiler_params=LIMIT,
        cost_estimate=cost(0.1, 5),
    )(length, q, g, o)


def own_stats(qs, own):
    return pl.pallas_call(
        own_stats_kernel,
        grid=(4,),
        in_specs=[per_head(1024, 128), own_block(0)],
        out_specs=per_head(16, 1024),
        out_shape=shape_of(4, 16, 1024, dtype=f32),
        scratch_shapes=[pltpu.VMEM((1024, 128), f32)],
        compiler_params=LIMIT,
        cost_estimate=cost(1.2, 6),
    )(qs, own)


def prefix(prompt, offset, qs, gs, st, delta, mine, other, pq, pg, po, HP=1):
    def heads(*shape):
        return pl.BlockSpec((HP,) + shape, lambda h: (h, 0, 0))

    big = pl.BlockSpec((8, 2 * HP, 32, 128), lambda h: (0, h, 0, 0))
    row = pl.BlockSpec((2, 1024 * HP), lambda h: (0, h))
    return pl.pallas_call(
        functools.partial(prefix_kernel, HP),
        grid=(4 // HP,),
        in_specs=[SMEM, SMEM, heads(1024, 128), heads(1024, 128), heads(16, 1024), heads(8, 1024), big, big, row, row, row],
        out_specs=[pl.BlockSpec((8, 2, 2 * HP, 32, 128), lambda h: (0, 0, h, 0, 0)), heads(128, 1024), heads(8, 1024), row],
        out_shape=[shape_of(8, 2, 8, 32, 128), shape_of(4, 128, 1024, dtype=f32),
                   shape_of(4, 8, 1024, dtype=f32), shape_of(2, 4096)],
        scratch_shapes=[pltpu.VMEM((512, 128), f32), pltpu.VMEM((512, 128), f32)],
        compiler_params=LIMIT,
        cost_estimate=cost(2.7, 8),
    )(prompt, offset, qs, gs, st, delta, mine, other, pq, pg, po)


def own_grads(qs, gs, delta, lse, dqt, own, CH=1024):
    return pl.pallas_call(
        functools.partial(own_grads_kernel, CH),
        grid=(4,),
        in_specs=[per_head(1024, 128), per_head(1024, 128), per_head(8, 1024), per_head(8, 1024), per_head(128, 1024),
                  own_block(0), own_block(1)],
        out_specs=[wide(128), pl.BlockSpec((8, 256, 128), lambda h: (0, h, 0))],
        out_shape=[shape_of(128, 4096), shape_of(8, 1024, 128)],
        scratch_shapes=[pltpu.VMEM((1024, 128), f32)] * 3,
        compiler_params=LIMIT,
        cost_estimate=cost(5.4, 10),
    )(qs, gs, delta, lse, dqt, own, own)


def copies_kernel(key_ref, value_ref, pack_key_ref, pack_value_ref, out_ref, pack_ref, block, rows, sems):
    taken = [pltpu.make_async_copy(pack_key_ref, rows.at[0], sems.at[16]), pltpu.make_async_copy(pack_value_ref, rows.at[1], sems.at[17])]
    for h in range(4):
        for kv, ref in enumerate((key_ref, value_ref)):
            i = 2 * h + kv
            source = ref.at[:, pl.ds(h * 128, 128)]
            taken.append(pltpu.make_async_copy(source, block.at[pl.ds(i * 128, 128)], sems.at[8 + i]))
    for copy in taken:
        copy.start()
    for copy in taken:
        copy.wait()
    sent = [pltpu.make_async_copy(block, out_ref.at[i], sems.at[i]) for i in range(8)]
    for copy in sent:
        copy.start()
    both = rows[...].astype(f32)
    parts = [both[kv][:, h * 128 : h * 128 + 128] for h in range(4) for kv in range(2)]
    pack_ref[...] = jnp.concatenate(parts, axis=0).astype(bf)
    for copy in sent:
        copy.wait()


def copies_of(key, value, pack_key, pack_value):
    return pl.pallas_call(
        copies_kernel,
        in_specs=[pl.BlockSpec(memory_space=pltpu.HBM)] * 4,
        out_specs=[pl.BlockSpec(memory_space=pl.ANY), pl.BlockSpec(memory_space=pltpu.VMEM)],
        out_shape=[shape_of(8, 1024, 128), shape_of(16, 128)],
        scratch_shapes=[pltpu.VMEM((1024, 128), bf), pltpu.VMEM((2, 2, 512), bf), pltpu.SemaphoreType.DMA((18,))],
        compiler_params=LIMIT,
        cost_estimate=cost(0, 2),
    )(key, value, pack_key, pack_value)


def regroup_kernel(*refs):
    x = jnp.concatenate([ref[...].astype(f32) for ref in refs[:-1]], axis=0)
    for k in range(8):
        blocks = [(i >> 3) | ((i & 7) << 1) for i in range(16)]
        rows = [x[16 * i + 2 * k : 16 * i + 2 * k + 2] for i in blocks]
        rows = jnp.concatenate(rows, axis=0).astype(bf)
        for c in range(8):
            refs[-1][c, k] = rows


def regroup(*blocks):
    return pl.pallas_call(
        regroup_kernel,
        out_shape=shape_of(8, 8, 32, 128),
        compiler_params=SMALL,
        cost_estimate=cost(0, 1),
    )(*blocks)


def ungroup_kernel(parts_ref, *refs):
    total = jnp.sum(parts_ref[...].astype(f32), axis=0)
    for m in range(4):
        rows = [total[s, k, 8 * i + 2 * m : 8 * i + 2 * m + 2] for s in range(2) for i in range(4) for k in range(8)]
        refs[m][...] = jnp.concatenate(rows, axis=0).astype(bf)


def ungroup(parts):
    return pl.pallas_call(
        ungroup_kernel,
        out_shape=[shape_of(128, 128)] * 4,
        compiler_params=SMALL,
        cost_estimate=cost(0, 1),
    )(parts)


def quarter_kernel(*refs):
    total = sum(ref[...].astype(f32) for ref in refs[:4])
    for m in range(4):
        both = [total[i : i + 16] for i in (16 * m, 64 + 16 * m)]
        refs[4 + m][...] = jnp.concatenate(both, axis=0).astype(bf)


def quarter(*blocks):
    return pl.pallas_call(
        quarter_kernel,
        out_shape=[shape_of(32, 128)] * 4,
        compiler_params=SMALL,
        cost_estimate=cost(0, 0.1),
    )(*blocks)


def sides_kernel(a_ref, b_ref, c_ref, d_ref, mine_ref, other_ref):
    total = sum(ref[...].astype(f32) for ref in (a_ref, b_ref, c_ref, d_ref))
    mine_ref[...] = total[0:16].astype(bf)
    other_ref[...] = total[16:32].astype(bf)


def sides(*blocks):
    return pl.pallas_call(
        sides_kernel, out_shape=[shape_of(16, 128)] * 2, compiler_params=SMALL, cost_estimate=cost(0, 0.1)
    )(*blocks)


def finish_pack_kernel(a_ref, b_ref, key_ref, value_ref):
    rows = a_ref[...].astype(f32) + b_ref[...].astype(f32)
    key_ref[...] = jnp.concatenate([rows[4 * h : 4 * h + 2] for h in range(4)], axis=1).astype(bf)
    value_ref[...] = jnp.concatenate([rows[4 * h + 2 : 4 * h + 4] for h in range(4)], axis=1).astype(bf)


def finish_pack(*blocks):
    return pl.pallas_call(
        finish_pack_kernel, out_shape=[shape_of(2, 512)] * 2, compiler_params=SMALL, cost_estimate=cost(0, 0.1)
    )(*blocks)


def finish_own_kernel(parts_ref, key_ref, value_ref):
    total = jnp.sum(parts_ref[...].astype(f32), axis=0)
    key_ref[...] = total[0:128].astype(bf)
    value_ref[...] = total[128:256].astype(bf)


def finish_own(parts):
    column = pl.BlockSpec((128, 128), lambda h: (0, h))
    return pl.pallas_call(
        finish_own_kernel,
        grid=(4,),
        in_specs=[pl.BlockSpec((8, 256, 128), lambda h: (0, h, 0))],
        out_specs=[column, column],
        out_shape=[shape_of(128, 512), shape_of(128, 512)],
        compiler_params=SMALL,
        cost_estimate=cost(0, 3),
    )(parts)


def from_partner(block, mask):
    return lax.ppermute(block, "resp", [(i, i ^ mask) for i in range(32)])


def exchange(blocks):
    return lax.all_to_all(blocks, "ctx", 0, 0, tiled=True)


def shards(
    resp_query, resp_key, resp_value, resp_out, resp_grad,
    pack_query, pack_key, pack_value, pack_out, pack_grad,
    resp_length, prompt_id, pack_offset,
):
    copies, block = copies_of(resp_key[0], resp_value[0], pack_key, pack_value)
    own = exchange(copies)
    for mask in (16, 2, 4):
        block = jnp.concatenate([block, from_partner(block, mask)], axis=0)
    block, q, g, o = lax.optimization_barrier((block, resp_query[0], resp_grad[0], resp_out[0]))
    qs, gs, delta = prepare(resp_length, q, g, o)
    last, qs = lax.optimization_barrier((from_partner(block, 8), qs))
    mine = exchange(regroup(block, last))
    st = own_stats(qs, own)
    mine, st = lax.optimization_barrier((mine, st))
    other = from_partner(mine, 1)
    d, dqt, lse, pdq = prefix(
        prompt_id, pack_offset, qs, gs, st, delta, mine, other, pack_query, pack_grad, pack_out
    )
    parts = exchange(d)
    dq, down = own_grads(qs, gs, delta, lse, dqt, own)
    parts = ungroup(parts)
    own_parts = exchange(down)
    parts = quarter(parts[0], *[from_partner(parts[m], 2 * m) for m in (1, 2, 3)])
    mine, other = sides(parts[0], *[from_partner(parts[m], 8 * m) for m in (1, 2, 3)])
    key, value = finish_own(own_parts)
    mine, key = lax.optimization_barrier((mine, key))
    block_key, block_value = finish_pack(mine, from_partner(other, 1))
    return dq[None], key[None], value[None], pdq, block_key, block_value


def solution(mesh):
    long = P("resp", "ctx", None)
    pack = P(("ctx", "resp"), None)
    return jax.shard_map(
        shards,
        mesh=mesh,
        in_specs=(long,) * 5 + (pack,) * 5 + (P("resp"), P("resp"), P()),
        out_specs=(long,) * 3 + (pack,) * 3,
        check_vma=False,
    )
```
